256 devices in a mesh: row: 16 (over y, z_lo, core), col: 16 (over x, z_hi).
Axes of the slice: x: 4, y: 4, z: 8 (z_hi: 4, z_lo: 2; z = z_hi * 2 + z_lo), core: 2. Of those that a mesh axis runs over, the one named last changes fastest.
Arguments:
- genotypes: int32 [18432, 512], P(('row', 'col')), may hold values from 0 to 2, as said below
- allele_counts: int32 [512], replicated, may hold values from 2168 to 106248
- relatedness: float32 [18432, 18432], P('row', 'col'), may hold values from -0.3 to 0.3
- protein_traits: float32 [18432, 128], P(('row', 'col')), may hold values from -6 to 6
Outputs:
- relatedness_out: float32 [18432, 18432], P('row', 'col')
- projected: float32 [18432, 128], P(('row', 'col'))
- cross_products: float32 [128, 128], replicated
The draws below stay inside these ranges and needn't reach their ends.
Inputs may be any that keep to these rules, and one draw needn't show every extreme that they name: `genotypes`: each dosage is the number of two independent draws that carry the alternative allele, each with the SNP's frequency.
All inputs are finite; a program needn't handle non-finite values.
Results may differ from the reference program's by a relative error of at most 0.00014.
Values sent between devices are 32-bit elements; how exact they have to be, the bound alone decides.
A program may use at most 64 MiB of HBM per device.

```python
import math
import jax
import jax.numpy as jnp
from jax import lax

SNPS = 512
PROT = 128
COHORT = 54208
SAMPLES = 18432
N_ROW = 16


def shared_counts(key):
    return jax.random.randint(key, (SNPS,), COHORT // 25, 2 * COHORT - COHORT // 25 + 1).astype(jnp.int32)


def draw_allele_counts(key, part):
    return shared_counts(key)


def draw_genotypes(key, part):
    counts = shared_counts(key)
    key = jax.random.fold_in(key, 2)
    first_key, second_key = jax.random.split(key)
    first = jax.random.randint(first_key, (SAMPLES, SNPS), 0, 2 * COHORT)
    second = jax.random.randint(second_key, (SAMPLES, SNPS), 0, 2 * COHORT)
    return (first < counts).astype(jnp.int32) + (second < counts).astype(jnp.int32)


def steps_of(own_key, shape, cuts, low, top_value):
    gain = 1.0
    for position, shards_of in cuts:
        steps = jax.random.uniform(jax.random.fold_in(jax.random.fold_in(own_key, 6), position), (shards_of,), jnp.float32, low / len(cuts), top_value / len(cuts))
        gain = gain * jnp.repeat(jnp.exp(steps), shape[position] // shards_of).reshape((-1,) + (1,) * (len(shape) - 1 - position))
    return gain


def centred(own_key, dims, scale, most, cuts=(), kind=jnp.bfloat16):
    loudness = steps_of(own_key, dims, cuts, -0.22, 0.18) if cuts else 1.0
    values = jax.random.normal(own_key, dims, jnp.float32) * scale * loudness
    return jnp.minimum(jnp.maximum(values, -most), most).astype(kind)


def setup_inputs(seed: int = 0) -> dict:
    key_of = jax.random.split(jax.random.key(seed), 5)
    genotypes = draw_genotypes(jax.random.fold_in(key_of[4], 71), 0)
    allele_counts = draw_allele_counts(jax.random.fold_in(key_of[4], 71), 0)
    relatedness = centred(key_of[2], (SAMPLES, SAMPLES), 0.05, 0.3, ((0, 16), (1, 16)), jnp.float32)
    protein_traits = centred(key_of[3], (SAMPLES, PROT), 1.0, 6.0, ((0, 256),), jnp.float32)
    return {"genotypes": genotypes, "allele_counts": allele_counts, "relatedness": relatedness, "protein_traits": protein_traits}


def standardize(genotypes, allele_counts):
    frequency = allele_counts.astype(jnp.float32) / (2.0 * COHORT)
    spread = lax.rsqrt(2.0 * frequency * (1.0 - frequency))
    return (genotypes.astype(jnp.float32) - 2.0 * frequency) * spread

def reference(genotypes, allele_counts, relatedness, protein_traits):
    scores = standardize(genotypes, allele_counts)

    def one_block(pair):
        rel_rows, score_rows = pair
        updated = rel_rows + lax.dot_general(score_rows, scores, (((1,), (1,)), ((), ())), precision=lax.Precision.HIGHEST, preferred_element_type=jnp.float32) / SNPS
        product = jnp.dot(updated, protein_traits, precision=lax.Precision.HIGHEST, preferred_element_type=jnp.float32)
        return (updated, product)
    updated, product = lax.map(one_block, (relatedness.reshape(N_ROW, -1, SAMPLES), scores.reshape(N_ROW, -1, SNPS)))
    updated = updated.reshape(SAMPLES, SAMPLES)
    product = product.reshape(SAMPLES, PROT)
    projected = product * math.sqrt(SNPS / SAMPLES)
    cross_products = lax.dot_general(protein_traits, product, (((0,), (0,)), ((), ())), precision=lax.Precision.HIGHEST, preferred_element_type=jnp.float32) / SAMPLES
    return (updated, projected, cross_products)
```

```python
import itertools
import math

import jax
import jax.numpy as jnp
from jax import lax
from jax.experimental import pallas as pl
from jax.experimental.pallas import tpu as pltpu
from jax.sharding import PartitionSpec as P

SNPS = 512
PROT = 128
COHORT = 54208
ROWS = 72
TOP = 40
GROUP = 4 * ROWS
PANEL = 16 * ROWS
SAMPLES = 16 * PANEL
MESH = pl.DeviceIdType.MESH
HIGHEST = lax.Precision.HIGHEST
F32 = jnp.float32
BF16 = jnp.bfloat16
NSEM = 128


def dot(a, b, contract, precision=None):
    return lax.dot_general(
        a, b, (contract, ((), ())), precision=precision, preferred_element_type=F32
    )


def split(value):
    high = value.astype(BF16)
    return high, (value - high.astype(F32)).astype(BF16)


def aligned(start, size, unit=8):
    return pl.ds(pl.multiple_of(start, unit), size)


def snp_tables(counts):
    frequency = counts.astype(F32) / (2.0 * COHORT)
    spread = lax.rsqrt(2.0 * frequency * (1.0 - frequency))
    return frequency, spread


def exchange_kernel(
    counts_ref,
    geno_ref,
    traits_ref,
    rel_ref,
    high_ref,
    low_ref,
    shift_ref,
    plain_ref,
    product_ref,
    cross_ref,
    rowp,
    colp,
    tp,
    rel,
    zbuf,
    zsum,
    rsx,
    rsz,
    gsrc,
    gk,
    ga,
    g7,
    gz,
    gx,
    gres,
    csrc,
    ck,
    ca,
    c7,
    cz,
    cx,
    cres,
    ssem,
    rsem,
    lsem,
):
    r = lax.axis_index("row")
    c = lax.axis_index("col")
    y, zl, core = r // 4, (r // 2) % 2, r % 2
    x, zh = c // 4, c % 4

    def row_of(y_, zl_, core_):
        return y_ * 4 + zl_ * 2 + core_

    def at_x(step):
        return (r, ((x + step) % 4) * 4 + zh)

    def at_z(step):
        return (r, x * 4 + (zh + step) % 4)

    def at_y(dy, dl):
        return (row_of((y + dy) % 4, (zl + dl) % 2, core), c)

    sibling = (row_of(y, zl, 1 - core), c)
    mirror = (c, r)
    others = [(dy, dl) for dl in range(2) for dy in range(4) if (dy, dl) != (0, 0)]
    partners = (
        [sibling]
        + [at_y(dy, dl) for dy, dl in others]
        + [at_x(i) for i in (1, 2, 3)]
        + [at_z(i) for i in (1, 2, 3)]
    )
    far = r != c

    names = itertools.count()
    started = []

    def copy(number, src, dst, to):
        return pltpu.make_async_remote_copy(
            src_ref=src,
            dst_ref=dst,
            send_sem=ssem.at[number],
            recv_sem=rsem.at[number],
            device_id=to,
            device_id_type=MESH,
        )

    def send(src, dst, to):
        number = next(names)
        moved = copy(number, src, dst, to)
        moved.start()
        started.append(moved)
        return number

    def arrived(number, landing):
        copy(number, landing, landing, sibling).wait_recv()

    load_rel = pltpu.make_async_copy(rel_ref, rel, lsem.at[0])
    load_rel.start()
    keep_own = pltpu.make_async_copy(geno_ref, rowp.at[c], lsem.at[1])
    keep_own.start()

    barrier = pltpu.get_barrier_semaphore()
    for to in partners:
        pl.semaphore_signal(barrier, inc=1, device_id=to, device_id_type=MESH)

    @pl.when(far)
    def _():
        pl.semaphore_signal(barrier, inc=1, device_id=mirror, device_id_type=MESH)

    frequency, spread = snp_tables(counts_ref[...])
    scores = (geno_ref[...].astype(F32) - 2.0 * frequency) * spread
    gsrc[...] = dot(traits_ref[...], scores, ((0,), (0,)), HIGHEST)

    pl.semaphore_wait(barrier, len(partners) + far.astype(jnp.int32))

    m_traits, m_geno = next(names), next(names)

    @pl.when(far)
    def _():
        copy(m_traits, traits_ref, tp.at[c], mirror).start()
        copy(m_geno, geno_ref, colp.at[c], mirror).start()

    @pl.when(jnp.logical_not(far))
    def _():
        for src, dst, sem in ((traits_ref, tp.at[c], 2), (geno_ref, colp.at[c], 3)):
            pltpu.make_async_copy(src, dst, lsem.at[sem]).start()

    def mirrored(number, src, landing, sem):
        @pl.when(far)
        def _():
            moved = copy(number, src, landing, mirror)
            moved.wait_recv()

        @pl.when(jnp.logical_not(far))
        def _():
            pltpu.make_async_copy(src, landing, lsem.at[sem]).wait()

    class Total:
        def __init__(self, src, bk, acc, b7, bz, bx, res, halves):
            self.src, self.bk, self.acc, self.b7 = src, bk, acc, b7
            self.bz, self.bx, self.res = bz, bx, res
            self.halves = halves
            self.rows = 64 if halves else 128
            self.chunk = self.rows // 8
            self.base = core * 64 if halves else 0

        def part(self, index):
            return aligned(index * self.chunk, self.chunk)

        def to_core(self):
            first = (1 - core) * 64 if self.halves else 0
            self.n_core = send(self.src.at[aligned(first, self.rows)], self.bk, sibling)

        def to_row(self):
            arrived(self.n_core, self.bk)
            mine = self.src[aligned(self.base, self.rows), :]
            self.acc[...] = mine + self.bk[...]
            me = y * 2 + zl
            self.n_row = []
            for dy, dl in others:
                q = ((y + dy) % 4) * 2 + (zl + dl) % 2
                self.n_row.append(
                    send(self.acc.at[self.part(q)], self.b7.at[me], at_y(dy, dl))
                )

        def to_z(self):
            me = y * 2 + zl
            for number in self.n_row:
                arrived(number, self.b7.at[me])
            self.b7[me] = self.acc[self.part(me), :]
            total = self.b7[0]
            for i in range(1, 8):
                total = total + self.b7[i]
            self.bz[zh] = total
            self.n_z = [send(self.bz.at[zh], self.bz.at[zh], at_z(i)) for i in (1, 2, 3)]

        def to_x(self):
            for number in self.n_z:
                arrived(number, self.bz.at[zh])
            total = (self.bz[0] + self.bz[1]) + (self.bz[2] + self.bz[3])
            self.bx[x] = total
            self.n_x = [send(self.bx.at[x], self.bx.at[x], at_x(i)) for i in (1, 2, 3)]

        def back_row(self):
            for number in self.n_x:
                arrived(number, self.bx.at[x])
            total = (self.bx[0] + self.bx[1]) + (self.bx[2] + self.bx[3])
            me = y * 2 + zl
            mine = aligned(self.base + me * self.chunk, self.chunk)
            self.res[mine, :] = total
            self.n_back = [
                send(self.res.at[mine], self.res.at[mine], at_y(dy, dl)) for dy, dl in others
            ]

        def back_core(self):
            me = y * 2 + zl
            mine = aligned(self.base + me * self.chunk, self.chunk)
            for number in self.n_back:
                arrived(number, self.res.at[mine])
            if self.halves:
                half = aligned(self.base, 64)
                self.n_half = send(self.res.at[half], self.res.at[half], sibling)

        def done(self):
            if self.halves:
                arrived(self.n_half, self.res.at[aligned(self.base, 64)])

    gram = Total(gsrc, gk, ga, g7, gz, gx, gres, True)
    cross = Total(csrc, ck, ca, c7, cz, cx, cres, False)

    def slot(x_step, z_step):
        return ((x + x_step) % 4) * 4 + (zh + z_step) % 4

    n_zup = send(geno_ref, rowp.at[c], at_z(1))
    n_zdown = send(geno_ref, rowp.at[c], at_z(3))
    n_xup, n_xdown = {}, {}

    def x_send(k, src):
        there = rowp.at[slot(0, k)]
        n_xup[k] = send(src, there, at_x(1))
        n_xdown[k] = send(src, there, at_x(3))

    x_send(0, geno_ref)
    gram.to_core()

    n_xfup, n_xfdown = {}, {}

    def x_forward(k):
        low = rowp.at[slot(3, k)]
        arrived(n_xup[k], low)
        n_xfup[k] = send(low.at[0:TOP], low.at[0:TOP], at_x(1))
        high = rowp.at[slot(1, k)]
        arrived(n_xdown[k], high)
        n_xfdown[k] = send(high.at[TOP:ROWS], high.at[TOP:ROWS], at_x(3))

    def x_last(k):
        opposite = rowp.at[slot(2, k)]
        arrived(n_xfup[k], opposite.at[0:TOP])
        arrived(n_xfdown[k], opposite.at[TOP:ROWS])

    def cslot(dy, dl, other=0):
        return row_of((y + dy) % 4, (zl + dl) % 2, (core + other) % 2)

    n_yup, n_ydown, n_yfup, n_yfdown, n_pair = {}, {}, {}, {}, {}

    def pair_send(dy, dl):
        block = colp.at[cslot(dy, dl)]
        n_pair[dy, dl] = send(block, block, sibling)

    def y_send(dl):
        block = colp.at[cslot(0, dl)]
        n_yup[dl] = send(block, block, at_y(1, 0))
        n_ydown[dl] = send(block, block, at_y(3, 0))
        pair_send(0, dl)

    def y_forward(dl):
        low = colp.at[cslot(3, dl)]
        arrived(n_yup[dl], low)
        n_yfup[dl] = send(low.at[0:TOP], low.at[0:TOP], at_y(1, 0))
        high = colp.at[cslot(1, dl)]
        arrived(n_ydown[dl], high)
        n_yfdown[dl] = send(high.at[TOP:ROWS], high.at[TOP:ROWS], at_y(3, 0))
        pair_send(3, dl)
        pair_send(1, dl)

    def y_last(dl):
        opposite = colp.at[cslot(2, dl)]
        arrived(n_yfup[dl], opposite.at[0:TOP])
        arrived(n_yfdown[dl], opposite.at[TOP:ROWS])
        pair_send(2, dl)

    mirrored(m_traits, traits_ref, tp.at[r], 2)
    n_t = [send(tp.at[r], tp.at[r], at_y(dy, dl)) for dy, dl in others]
    n_tp = {(0, 0): send(tp.at[r], tp.at[r], sibling)}

    gram.to_row()

    mirrored(m_geno, geno_ref, colp.at[r], 3)
    n_zl = send(colp.at[r], colp.at[r], at_y(0, 1))
    y_send(0)

    low = rowp.at[slot(0, 3)]
    arrived(n_zup, low)
    n_zfup = send(low.at[0:TOP], low.at[0:TOP], at_z(1))
    x_send(3, low)
    high = rowp.at[slot(0, 1)]
    arrived(n_zdown, high)
    n_zfdown = send(high.at[TOP:ROWS], high.at[TOP:ROWS], at_z(3))
    x_send(1, high)

    for number, (dy, dl) in zip(n_t, others, strict=True):
        block = tp.at[cslot(-dy, -dl)]
        arrived(number, block)
        n_tp[-dy % 4, dl] = send(block, block, sibling)

    gram.to_z()

    arrived(n_zl, colp.at[cslot(0, 1)])
    y_send(1)
    x_forward(0)

    for (dy, dl), number in n_tp.items():
        arrived(number, tp.at[cslot(dy, dl, 1)])
    load_rel.wait()
    t_all = tp[...].reshape(PANEL, PROT)
    t_high, t_low = split(t_all)
    t_both = jnp.concatenate([t_high, t_low], axis=1)

    def times_traits(step, _):
        there = (x + step) % 4
        rows = aligned(there * GROUP, GROUP)
        r_high, r_low = split(rel[rows, :])
        both = dot(r_high, t_both, ((1,), (0,)))
        zbuf[rows, :] = (
            both[:, :PROT] + both[:, PROT:] + dot(r_low, t_high, ((1,), (0,)))
        )
        return 0

    lax.fori_loop(0, 4, times_traits, 0)
    n_rsx = []
    for i in (1, 2, 3):
        rows = aligned(((x + i) % 4) * GROUP, GROUP)
        n_rsx.append(send(zbuf.at[rows], rsx.at[x], at_x(i)))

    opposite = rowp.at[slot(0, 2)]
    arrived(n_zfup, opposite.at[0:TOP])
    arrived(n_zfdown, opposite.at[TOP:ROWS])
    x_send(2, opposite)
    y_forward(0)
    y_forward(1)
    gram.to_x()
    x_forward(3)
    x_forward(1)
    y_last(0)
    y_last(1)

    rsx[x] = zbuf[aligned(x * GROUP, GROUP), :]
    for number in n_rsx:
        arrived(number, rsx.at[x])
    summed = (rsx[0] + rsx[1]) + (rsx[2] + rsx[3])
    zsum[...] = summed
    n_rsz = []
    for i in (1, 2, 3):
        rows = aligned(((zh + i) % 4) * ROWS, ROWS)
        n_rsz.append(send(zsum.at[rows], rsz.at[zh], at_z(i)))
    rsz[zh] = zsum[aligned(zh * ROWS, ROWS), :]

    gram.back_row()
    x_forward(2)
    for dl in range(2):
        for dy in range(4):
            arrived(n_pair[dy, dl], colp.at[cslot(dy, dl, 1)])
    gram.back_core()

    for number in n_rsz:
        arrived(number, rsz.at[zh])
    own = (rsz[0] + rsz[1]) + (rsz[2] + rsz[3])
    csrc[...] = dot(traits_ref[...], own, ((0,), (0,)), HIGHEST)
    cross.to_core()

    keep_own.wait()
    nearest = jnp.round(2.0 * frequency)
    offset = 2.0 * frequency - nearest
    weight = spread * spread * (1.0 / SNPS)

    def plain(step, _):
        block = colp[pl.ds(4 * step, 4)].reshape(GROUP, SNPS).astype(F32)
        plain_ref[aligned(step * GROUP, GROUP, 16), :] = (block - nearest).astype(BF16)
        return 0

    lax.fori_loop(0, 4, plain, 0)

    cross.to_row()

    def weighted(step):
        which = (x + step) % 4
        rows = aligned(which * GROUP, GROUP, 16)
        block = rowp[pl.ds(4 * which, 4)].reshape(GROUP, SNPS).astype(F32)
        value = ((block - nearest) - offset) * weight
        one, two = split(value)
        high_ref[rows, :] = one
        low_ref[rows, :] = two
        shift = jnp.sum(value * offset, axis=1, keepdims=True)
        shift_ref[rows, :] = jnp.broadcast_to(shift, (GROUP, PROT))

    weighted(0)
    cross.to_z()
    weighted(1)
    weighted(3)
    gram.done()
    cross.to_x()
    for k in (0, 3, 1, 2):
        x_last(k)
    weighted(2)
    cross.back_row()
    product_ref[...] = own + dot(scores, gres[...], ((1,), (1,)), HIGHEST) * (1.0 / SNPS)
    whole = gres[...]
    squares = dot(whole, whole, ((1,), (1,)), HIGHEST) * (1.0 / SNPS)
    cross.back_core()
    cross.done()
    cross_ref[...] = cres[...] + squares

    for moved in started:
        moved.wait_send()

    @pl.when(far)
    def _():
        copy(m_traits, traits_ref, tp.at[c], mirror).wait_send()
        copy(m_geno, geno_ref, colp.at[c], mirror).wait_send()


def update_kernel(
    rel_ref, high_ref, low_ref, shift_ref, plain_ref, product_ref, cross_ref, out_ref, proj_ref, cp_ref
):
    plain = plain_ref[...]
    sums = dot(high_ref[...], plain, ((1,), (1,))) + dot(low_ref[...], plain, ((1,), (1,)))
    out_ref[...] = rel_ref[...] + (sums - shift_ref[:, 0:1])
    proj_ref[...] = product_ref[...] * math.sqrt(SNPS / SAMPLES)
    cp_ref[...] = cross_ref[...] * (1.0 / SAMPLES)


def on_device(genotypes, allele_counts, relatedness, protein_traits):
    vmem = pl.BlockSpec(memory_space=pltpu.VMEM)
    anywhere = pl.BlockSpec(memory_space=pl.ANY)
    like = jax.ShapeDtypeStruct
    f32 = lambda *shape: pltpu.VMEM(shape, F32)
    high, low, shift, plain, product, cross = pl.pallas_call(
        exchange_kernel,
        out_shape=(
            like((PANEL, SNPS), BF16),
            like((PANEL, SNPS), BF16),
            like((PANEL, PROT), F32),
            like((PANEL, SNPS), BF16),
            like((ROWS, PROT), F32),
            like((PROT, PROT), F32),
        ),
        in_specs=[vmem, vmem, vmem, anywhere],
        out_specs=(vmem,) * 6,
        scratch_shapes=[
            pltpu.VMEM((16, ROWS, SNPS), jnp.int32),
            pltpu.VMEM((16, ROWS, SNPS), jnp.int32),
            f32(16, ROWS, PROT),
            f32(PANEL, PANEL),
            f32(PANEL, PROT),
            f32(GROUP, PROT),
            f32(4, GROUP, PROT),
            f32(4, ROWS, PROT),
            f32(128, SNPS),
            f32(64, SNPS),
            f32(64, SNPS),
            f32(8, 8, SNPS),
            f32(4, 8, SNPS),
            f32(4, 8, SNPS),
            f32(128, SNPS),
            f32(128, PROT),
            f32(128, PROT),
            f32(128, PROT),
            f32(8, 16, PROT),
            f32(4, 16, PROT),
            f32(4, 16, PROT),
            f32(128, PROT),
            pltpu.SemaphoreType.DMA((NSEM,)),
            pltpu.SemaphoreType.DMA((NSEM,)),
            pltpu.SemaphoreType.DMA((4,)),
        ],
        compiler_params=pltpu.CompilerParams(
            collective_id=1, has_side_effects=True, vmem_limit_bytes=48 * 2**20
        ),
        name="exchange",
    )(allele_counts.reshape(1, SNPS), genotypes, protein_traits, relatedness)
    steps = 4
    tile = PANEL // steps
    rows = lambda width: pl.BlockSpec((tile, width), lambda i: (i, 0))
    whole = lambda *shape: pl.BlockSpec(shape, lambda i: (0, 0))
    return pl.pallas_call(
        update_kernel,
        grid=(steps,),
        out_shape=(
            like((PANEL, PANEL), F32),
            like((ROWS, PROT), F32),
            like((PROT, PROT), F32),
        ),
        in_specs=[
            rows(PANEL),
            rows(SNPS),
            rows(SNPS),
            rows(PROT),
            whole(PANEL, SNPS),
            whole(ROWS, PROT),
            whole(PROT, PROT),
        ],
        out_specs=(rows(PANEL), whole(ROWS, PROT), whole(PROT, PROT)),
        compiler_params=pltpu.CompilerParams(vmem_limit_bytes=48 * 2**20),
        name="update",
    )(relatedness, high, low, shift, plain, product, cross)


def solution(mesh):
    in_specs = (P(("row", "col"), None), P(), P("row", "col"), P(("row", "col"), None))
    out_specs = (P("row", "col"), P(("row", "col"), None), P())
    return jax.shard_map(
        on_device, mesh=mesh, in_specs=in_specs, out_specs=out_specs, check_vma=False
    )
```

```python
import itertools
import math

import jax
import jax.numpy as jnp
from jax import lax
from jax.experimental import pallas as pl
from jax.experimental.pallas import tpu as pltpu
from jax.sharding import PartitionSpec as P

SNPS = 512
PROT = 128
COHORT = 54208
ROWS = 72
TOP = 40
GROUP = 4 * ROWS
PANEL = 16 * ROWS
SAMPLES = 16 * PANEL
MESH = pl.DeviceIdType.MESH
HIGHEST = lax.Precision.HIGHEST
F32 = jnp.float32
BF16 = jnp.bfloat16
NSEM = 160
STORES = 8
VMEM_LIMIT = 52 * 2**20
ORDER = (
    "g0", "t0", "z0", "m0", "t1", "g1", "x0", "z1d", "m1", "z1u", "t2", "t3", "m2t", "yf0u",
    "yf0d", "tz0", "g2", "m3t", "m1t", "m2", "yl0", "m0t", "g3", "z2", "t4", "yf1u", "tz1",
    "yf1d", "xf1u", "tc", "s0", "xf3u", "yl1", "g4", "xf0d", "s1", "p", "h", "xf2d", "xf3d",
    "xf2u", "g5", "u0", "xf0u", "u3", "xf1d", "g6", "og", "s2", "u1", "xl0", "xl2", "op", "xl1",
    "xl3", "u2", "s3", "oc",
)


def dot(a, b, contract, precision=None):
    return lax.dot_general(
        a, b, (contract, ((), ())), precision=precision, preferred_element_type=F32
    )


def split(value):
    high = value.astype(BF16)
    return high, (value - high.astype(F32)).astype(BF16)


def aligned(start, size, unit=8):
    return pl.ds(pl.multiple_of(start, unit), size)


def snp_tables(counts):
    frequency = counts.astype(F32) / (2.0 * COHORT)
    spread = lax.rsqrt(2.0 * frequency * (1.0 - frequency))
    return frequency, spread


def exchange_kernel(
    counts_ref,
    geno_ref,
    traits_ref,
    rel_ref,
    rel,
    projected_ref,
    cross_ref,
    counts,
    traits,
    rowp,
    colp,
    tp,
    tr,
    turned,
    tb,
    zbuf,
    zsum,
    rsx,
    rsz,
    gsrc,
    gk,
    ga,
    g7,
    gz,
    gx,
    gres,
    csrc,
    c16,
    cc,
    cres,
    ssem,
    rsem,
    lsem,
):
    r = lax.axis_index("row")
    c = lax.axis_index("col")
    y, zl, core = r // 4, (r // 2) % 2, r % 2
    x, zh = c // 4, c % 4

    def row_of(y_, zl_, core_):
        return y_ * 4 + zl_ * 2 + core_

    def at_x(step):
        return (r, ((x + step) % 4) * 4 + zh)

    def at_z(step):
        return (r, x * 4 + (zh + step) % 4)

    def at_y(dy, dl):
        return (row_of((y + dy) % 4, (zl + dl) % 2, core), c)

    sibling = (row_of(y, zl, 1 - core), c)
    mirror = (c, r)
    others = [(dy, dl) for dl in range(2) for dy in range(4) if (dy, dl) != (0, 0)]

    def at_row(dy, dl, dk):
        return (row_of((y + dy) % 4, (zl + dl) % 2, (core + dk) % 2), c)

    def at_col(dx, dz):
        return (r, ((x + dx) % 4) * 4 + (zh + dz) % 4)

    row_others = [
        (dy, dl, dk) for dk in range(2) for dl in range(2) for dy in range(4)
    ][1:]
    col_others = [(dx, dz) for dz in range(4) for dx in range(4)][1:]
    partners = [at_row(*d) for d in row_others] + [at_col(*d) for d in col_others]
    far = r != c

    names = itertools.count()
    started = []

    def copy(number, src, dst, to):
        return pltpu.make_async_remote_copy(
            src_ref=src,
            dst_ref=dst,
            send_sem=ssem.at[number],
            recv_sem=rsem.at[number],
            device_id=to,
            device_id_type=MESH,
        )

    def send(src, dst, to):
        number = next(names)
        moved = copy(number, src, dst, to)
        moved.start()
        started.append(moved)
        return number

    def arrived(number, landing):
        copy(number, landing, landing, sibling).wait_recv()

    load_counts = pltpu.make_async_copy(counts_ref, counts, lsem.at[4])
    load_counts.start()
    load_traits = pltpu.make_async_copy(traits_ref, traits, lsem.at[5])
    load_traits.start()
    keep_own = pltpu.make_async_copy(geno_ref, rowp.at[c], lsem.at[1])
    keep_own.start()
    load_rel = pltpu.make_async_copy(rel_ref, rel, lsem.at[0])
    load_rel.start()

    barrier = pltpu.get_barrier_semaphore()
    for to in partners:
        pl.semaphore_signal(barrier, inc=1, device_id=to, device_id_type=MESH)

    @pl.when(far)
    def _():
        pl.semaphore_signal(barrier, inc=1, device_id=mirror, device_id_type=MESH)

    load_counts.wait()
    frequency, spread = snp_tables(counts[...])
    nearest = jnp.round(2.0 * frequency)
    offset = 2.0 * frequency - nearest
    weight = spread * spread * (1.0 / SNPS)
    keep_own.wait()
    load_traits.wait()
    scores = (rowp[c].astype(F32) - 2.0 * frequency) * spread
    gsrc[...] = dot(traits[...], scores, ((0,), (0,)), HIGHEST)

    pl.semaphore_wait(barrier, len(partners) + far.astype(jnp.int32))

    steps = {}

    def step(function):
        steps[function.__name__] = function

    m_traits, m_geno = next(names), next(names)
    mirrors = {
        "t": (m_traits, traits_ref, lambda i: tp.at[i], 2),
        "c": (m_geno, geno_ref, lambda i: cblock(i), 3),
    }

    def cblock(index):
        return colp.at[aligned(index * ROWS, ROWS)]

    def mirror_start(which):
        number, src, panel, sem = mirrors[which]

        @pl.when(far)
        def _():
            copy(number, src, panel(c), mirror).start()

        @pl.when(jnp.logical_not(far))
        def _():
            pltpu.make_async_copy(src, panel(c), lsem.at[sem]).start()

    def mirrored(which):
        number, src, panel, sem = mirrors[which]

        @pl.when(far)
        def _():
            copy(number, src, panel(r), mirror).wait_recv()

        @pl.when(jnp.logical_not(far))
        def _():
            pltpu.make_async_copy(src, panel(r), lsem.at[sem]).wait()

    def mirror_sent(which):
        number, src, panel, sem = mirrors[which]

        @pl.when(far)
        def _():
            copy(number, src, panel(c), mirror).wait_send()

    class Total:
        def __init__(self, src, bk, acc, b7, bz, bx, res, halves):
            self.src, self.bk, self.acc, self.b7 = src, bk, acc, b7
            self.bz, self.bx, self.res = bz, bx, res
            self.halves = halves
            self.rows = 64 if halves else 128
            self.chunk = self.rows // 8
            self.base = core * 64 if halves else 0

        def part(self, index):
            return aligned(index * self.chunk, self.chunk)

        def to_core(self):
            first = (1 - core) * 64 if self.halves else 0
            self.n_core = send(self.src.at[aligned(first, self.rows)], self.bk, sibling)

        def to_row(self):
            arrived(self.n_core, self.bk)
            mine = self.src[aligned(self.base, self.rows), :]
            self.acc[...] = mine + self.bk[...]
            me = y * 2 + zl
            self.n_row = []
            for dy, dl in others:
                q = ((y + dy) % 4) * 2 + (zl + dl) % 2
                self.n_row.append(
                    send(self.acc.at[self.part(q)], self.b7.at[me], at_y(dy, dl))
                )

        def to_z(self):
            me = y * 2 + zl
            for number in self.n_row:
                arrived(number, self.b7.at[me])
            self.b7[me] = self.acc[self.part(me), :]
            total = self.b7[0]
            for i in range(1, 8):
                total = total + self.b7[i]
            self.bz[zh] = total
            self.n_z = [send(self.bz.at[zh], self.bz.at[zh], at_z(i)) for i in (1, 2, 3)]

        def to_x(self):
            for number in self.n_z:
                arrived(number, self.bz.at[zh])
            total = (self.bz[0] + self.bz[1]) + (self.bz[2] + self.bz[3])
            self.bx[x] = total
            self.n_x = [send(self.bx.at[x], self.bx.at[x], at_x(i)) for i in (1, 2, 3)]

        def back_row(self):
            for number in self.n_x:
                arrived(number, self.bx.at[x])
            total = (self.bx[0] + self.bx[1]) + (self.bx[2] + self.bx[3])
            me = y * 2 + zl
            mine = aligned(self.base + me * self.chunk, self.chunk)
            self.res[mine, :] = total
            self.n_back = [
                send(self.res.at[mine], self.res.at[mine], at_y(dy, dl)) for dy, dl in others
            ]

        def back_core(self):
            me = y * 2 + zl
            mine = aligned(self.base + me * self.chunk, self.chunk)
            for number in self.n_back:
                arrived(number, self.res.at[mine])
            if self.halves:
                half = aligned(self.base, 64)
                self.n_half = send(self.res.at[half], self.res.at[half], sibling)

        def done(self):
            if self.halves:
                arrived(self.n_half, self.res.at[aligned(self.base, 64)])

    gram = Total(gsrc, gk, ga, g7, gz, gx, gres, True)

    class Quick:
        def __init__(self, src, by_row, by_col, res):
            self.src, self.by_row, self.by_col, self.res = src, by_row, by_col, res

        def part(self, index):
            return aligned(index * 8, 8)

        def to_row(self):
            self.n = []
            for d in row_others:
                there = at_row(*d)
                self.n.append(
                    send(self.src.at[self.part(there[0])], self.by_row.at[r], there)
                )
            self.by_row[r] = self.src[self.part(r), :]

        def to_col(self):
            for number in self.n:
                arrived(number, self.by_row.at[r])
            total = self.by_row[0]
            for i in range(1, 16):
                total = total + self.by_row[i]
            self.by_col[c] = total
            mine = self.by_col.at[c]
            self.n = [send(mine, mine, at_col(*d)) for d in col_others]

        def back(self):
            for number in self.n:
                arrived(number, self.by_col.at[c])
            total = self.by_col[0]
            for i in range(1, 16):
                total = total + self.by_col[i]
            self.res[self.part(r), :] = total
            mine = self.res.at[self.part(r)]
            self.n = [send(mine, mine, at_row(*d)) for d in row_others]

        def done(self):
            for number in self.n:
                arrived(number, self.res.at[self.part(r)])

    quick = Quick(csrc, c16, cc, cres)
    steps["s0"], steps["s1"], steps["s2"], steps["s3"] = (
        quick.to_row,
        quick.to_col,
        quick.back,
        quick.done,
    )
    for index, name in enumerate(
        ("to_core", "to_row", "to_z", "to_x", "back_row", "back_core", "done")
    ):
        steps[f"g{index}"] = getattr(gram, name)

    def slot(x_step, z_step):
        return ((x + x_step) % 4) * 4 + (zh + z_step) % 4

    n_z = {}
    n_xup, n_xdown, n_xfup, n_xfdown = {}, {}, {}, {}

    def x_send(k, src):
        there = rowp.at[slot(0, k)]
        n_xup[k] = send(src, there, at_x(1))
        n_xdown[k] = send(src, there, at_x(3))

    def x_up(k):
        low = rowp.at[slot(3, k)]
        arrived(n_xup[k], low)
        n_xfup[k] = send(low.at[0:TOP], low.at[0:TOP], at_x(1))

    def x_down(k):
        high = rowp.at[slot(1, k)]
        arrived(n_xdown[k], high)
        n_xfdown[k] = send(high.at[TOP:ROWS], high.at[TOP:ROWS], at_x(3))

    def x_last(k):
        opposite = rowp.at[slot(2, k)]
        arrived(n_xfup[k], opposite.at[0:TOP])
        arrived(n_xfdown[k], opposite.at[TOP:ROWS])

    for k in range(4):
        steps[f"xf{k}u"] = lambda k=k: x_up(k)
        steps[f"xf{k}d"] = lambda k=k: x_down(k)
        steps[f"xl{k}"] = lambda k=k: x_last(k)

    @step
    def z0():
        n_z["up"] = send(geno_ref, rowp.at[c], at_z(1))
        n_z["down"] = send(geno_ref, rowp.at[c], at_z(3))

    @step
    def x0():
        x_send(0, geno_ref)

    @step
    def z1u():
        low = rowp.at[slot(0, 3)]
        arrived(n_z["up"], low)
        n_z["fup"] = send(low.at[0:TOP], low.at[0:TOP], at_z(1))
        x_send(3, low)

    @step
    def z1d():
        high = rowp.at[slot(0, 1)]
        arrived(n_z["down"], high)
        n_z["fdown"] = send(high.at[TOP:ROWS], high.at[TOP:ROWS], at_z(3))
        x_send(1, high)

    @step
    def z2():
        opposite = rowp.at[slot(0, 2)]
        arrived(n_z["fup"], opposite.at[0:TOP])
        arrived(n_z["fdown"], opposite.at[TOP:ROWS])
        x_send(2, opposite)

    def cslot(dy, dl, other=0):
        return row_of((y + dy) % 4, (zl + dl) % 2, (core + other) % 2)

    n_yup, n_ydown, n_yfup, n_yfdown, n_pair = {}, {}, {}, {}, {}
    n_zl = []

    def pair_send(dy, dl):
        block = cblock(cslot(dy, dl))
        n_pair[dy, dl] = send(block, block, sibling)

    def y_send(dl):
        block = cblock(cslot(0, dl))
        n_yup[dl] = send(block, block, at_y(1, 0))
        n_ydown[dl] = send(block, block, at_y(3, 0))
        pair_send(0, dl)

    def y_up(dl):
        low = cblock(cslot(3, dl))
        arrived(n_yup[dl], low)
        n_yfup[dl] = send(low.at[0:TOP], low.at[0:TOP], at_y(1, 0))
        pair_send(3, dl)

    def y_down(dl):
        high = cblock(cslot(1, dl))
        arrived(n_ydown[dl], high)
        n_yfdown[dl] = send(high.at[TOP:ROWS], high.at[TOP:ROWS], at_y(3, 0))
        pair_send(1, dl)

    def y_last(dl):
        opposite = cblock(cslot(2, dl))
        arrived(n_yfup[dl], opposite.at[0:TOP])
        arrived(n_yfdown[dl], opposite.at[TOP:ROWS])
        pair_send(2, dl)

    for dl in range(2):
        steps[f"yf{dl}u"] = lambda dl=dl: y_up(dl)
        steps[f"yf{dl}d"] = lambda dl=dl: y_down(dl)
        steps[f"yl{dl}"] = lambda dl=dl: y_last(dl)

    @step
    def m0():
        mirror_start("c")

    @step
    def m1():
        mirrored("c")
        n_zl.append(send(cblock(r), cblock(r), at_y(0, 1)))
        y_send(0)

    @step
    def m2():
        arrived(n_zl[0], cblock(cslot(0, 1)))
        y_send(1)

    @step
    def p():
        for dl in range(2):
            for dy in range(4):
                arrived(n_pair[dy, dl], cblock(cslot(dy, dl, 1)))

    n_t, n_tp, n_tz = [], {}, []

    @step
    def t0():
        mirror_start("t")

    @step
    def tz0():
        for i in (1, 2, 3):
            n_tz.append(send(traits_ref, tr.at[zh], at_z(i)))
        tr[zh] = traits[...]

    @step
    def tz1():
        for number in n_tz:
            arrived(number, tr.at[zh])

    @step
    def t1():
        mirrored("t")
        for dy, dl in others:
            n_t.append(send(tp.at[r], tp.at[r], at_y(dy, dl)))
        n_tp[0, 0] = send(tp.at[r], tp.at[r], sibling)

    @step
    def t2():
        for number, (dy, dl) in zip(n_t, others, strict=True):
            block = tp.at[cslot(-dy, -dl)]
            arrived(number, block)
            n_tp[-dy % 4, dl] = send(block, block, sibling)

    n_rsx, n_rsz = [], []

    @step
    def t3():
        for (dy, dl), number in n_tp.items():
            arrived(number, tp.at[cslot(dy, dl, 1)])
        load_rel.wait()
        t_high, t_low = split(tp[...].reshape(PANEL, PROT))
        tb[:, :PROT] = t_high
        tb[:, PROT:] = t_low

    def times_traits(i):
        rows = aligned(((x + i) % 4) * GROUP, GROUP)
        r_high, r_low = split(rel[rows, :])
        both = dot(r_high, tb[...], ((1,), (0,)))
        product = both[:, :PROT] + both[:, PROT:] + dot(r_low, tb[:, :PROT], ((1,), (0,)))
        zbuf[rows, :] = product
        if i:
            n_rsx.append(send(zbuf.at[rows], rsx.at[x], at_x(i)))
        else:
            rsx[x] = product

    for i in range(4):
        steps[f"m{i}t"] = lambda i=i: times_traits(i)

    @step
    def t4():
        for number in n_rsx:
            arrived(number, rsx.at[x])
        zsum[...] = (rsx[0] + rsx[1]) + (rsx[2] + rsx[3])
        for i in (1, 2, 3):
            rows = aligned(((zh + i) % 4) * ROWS, ROWS)
            n_rsz.append(send(zsum.at[rows], rsz.at[zh], at_z(i)))
        rsz[zh] = zsum[aligned(zh * ROWS, ROWS), :]

    @step
    def tc():
        four = tr[...].reshape(GROUP, PROT)
        csrc[...] = dot(four, zsum[...], ((0,), (0,)), HIGHEST)

    @step
    def h():
        def plain(step, _):
            rows = aligned(step * 128, 128)
            block = (colp[rows, :].astype(F32) - nearest).T
            turned[:, rows] = block.astype(BF16)
            return 0

        lax.fori_loop(0, PANEL // 128, plain, 0)

    def update(i):
        which = (x + i) % 4
        rows = aligned(which * GROUP, GROUP)
        block = rowp[pl.ds(4 * which, 4)].reshape(GROUP, SNPS).astype(F32)
        value = ((block - nearest) - offset) * weight
        high, low = split(value)
        shift = jnp.sum(value * offset, axis=1, keepdims=True)
        sums = dot(high, turned[...], ((1,), (0,))) + dot(low, turned[...], ((1,), (0,)))
        rel[rows, :] = rel[rows, :] + (sums - shift)

    for k in range(4):
        steps[f"u{k}"] = lambda k=k: update(k)

    @step
    def op():
        for number in n_rsz:
            arrived(number, rsz.at[zh])
        own = (rsz[0] + rsz[1]) + (rsz[2] + rsz[3])
        product = own + dot(scores, gres[...], ((1,), (1,)), HIGHEST) * (1.0 / SNPS)
        projected_ref[...] = product * math.sqrt(SNPS / SAMPLES)

    @step
    def og():
        whole = gres[...]
        cross_ref[...] = dot(whole, whole, ((1,), (1,)), HIGHEST) * (1.0 / SNPS)

    @step
    def oc():
        cross_ref[...] = (cres[...] + cross_ref[...]) * (1.0 / SAMPLES)

    order = ORDER
    for name in order:
        steps[name]()

    for moved in started:
        moved.wait_send()
    mirror_sent("t")
    mirror_sent("c")


def store_kernel(updated_ref, projected_ref, cross_ref, out_ref, proj_ref, cp_ref, sem):
    tile = PANEL // STORES
    moves = [
        pltpu.make_async_copy(projected_ref, proj_ref, sem.at[STORES]),
        pltpu.make_async_copy(cross_ref, cp_ref, sem.at[STORES + 1]),
    ]
    for i in range(STORES):
        rows = pl.ds(i * tile, tile)
        moves.append(pltpu.make_async_copy(updated_ref.at[rows], out_ref.at[rows], sem.at[i]))
    for move in moves:
        move.start()
    for move in moves:
        move.wait()


def on_device(genotypes, allele_counts, relatedness, protein_traits):
    vmem = pl.BlockSpec(memory_space=pltpu.VMEM)
    anywhere = pl.BlockSpec(memory_space=pl.ANY)
    like = jax.ShapeDtypeStruct
    f32 = lambda *shape: pltpu.VMEM(shape, F32)
    updated, projected, cross = pl.pallas_call(
        exchange_kernel,
        out_shape=(f32(PANEL, PANEL), f32(ROWS, PROT), f32(PROT, PROT)),
        in_specs=[anywhere] * 4,
        out_specs=(vmem,) * 3,
        scratch_shapes=[
            pltpu.VMEM((1, SNPS), jnp.int32),
            f32(ROWS, PROT),
            pltpu.VMEM((16, ROWS, SNPS), jnp.int32),
            pltpu.VMEM((PANEL, SNPS), jnp.int32),
            f32(16, ROWS, PROT),
            f32(4, ROWS, PROT),
            pltpu.VMEM((SNPS, PANEL), BF16),
            pltpu.VMEM((PANEL, 2 * PROT), BF16),
            f32(PANEL, PROT),
            f32(GROUP, PROT),
            f32(4, GROUP, PROT),
            f32(4, ROWS, PROT),
            f32(128, SNPS),
            f32(64, SNPS),
            f32(64, SNPS),
            f32(8, 8, SNPS),
            f32(4, 8, SNPS),
            f32(4, 8, SNPS),
            f32(128, SNPS),
            f32(PROT, PROT),
            f32(16, 8, PROT),
            f32(16, 8, PROT),
            f32(PROT, PROT),
            pltpu.SemaphoreType.DMA((NSEM,)),
            pltpu.SemaphoreType.DMA((NSEM,)),
            pltpu.SemaphoreType.DMA((6,)),
        ],
        compiler_params=pltpu.CompilerParams(
            collective_id=1, has_side_effects=True, vmem_limit_bytes=VMEM_LIMIT
        ),
        name="exchange",
    )(allele_counts.reshape(1, SNPS), genotypes, protein_traits, relatedness)
    return pl.pallas_call(
        store_kernel,
        out_shape=(
            like((PANEL, PANEL), F32),
            like((ROWS, PROT), F32),
            like((PROT, PROT), F32),
        ),
        in_specs=[vmem] * 3,
        out_specs=(anywhere,) * 3,
        scratch_shapes=[pltpu.SemaphoreType.DMA((STORES + 2,))],
        compiler_params=pltpu.CompilerParams(vmem_limit_bytes=16 * 2**20),
        name="store",
    )(updated, projected, cross)


def solution(mesh):
    in_specs = (P(("row", "col"), None), P(), P("row", "col"), P(("row", "col"), None))
    out_specs = (P("row", "col"), P(("row", "col"), None), P())
    return jax.shard_map(
        on_device, mesh=mesh, in_specs=in_specs, out_specs=out_specs, check_vma=False
    )
```

```python
import itertools
import math

import jax
import jax.numpy as jnp
from jax import lax
from jax.experimental import pallas as pl
from jax.experimental.pallas import tpu as pltpu
from jax.sharding import PartitionSpec as P

SNPS = 512
PROT = 128
COHORT = 54208
ROWS = 72
TOP = 40
GROUP = 4 * ROWS
PANEL = 16 * ROWS
SAMPLES = 16 * PANEL
MESH = pl.DeviceIdType.MESH
HIGHEST = lax.Precision.HIGHEST
F32 = jnp.float32
BF16 = jnp.bfloat16
NSEM = 160
STORES = 8
VMEM_LIMIT = 52 * 2**20
ORDER = (
    "t0", "z0", "m0", "g0", "t1", "rs", "x0", "z1u", "g1", "x3s", "m1", "ys0", "t2a", "z1d",
    "x1s", "t2", "yf0d", "g2", "yf0u", "t3", "tz0", "m2t", "m1t", "m3t", "m2", "ys1", "yf1u",
    "xf1u", "yl0", "yf1d", "xf0d", "pp11", "pp20", "m0t", "tz1", "xf3d", "pp31", "pp00", "g3",
    "z2", "pp30", "pp01", "t4", "tc", "s0", "pp10", "yl1", "x2s", "g4", "pp21", "xf1d", "s1",
    "g5", "p", "xf0u", "h", "xl1", "xf3u", "xf2u", "u3", "g6", "op", "xf2d", "u1", "s2", "xl0",
    "u0", "og", "xl3", "xl2", "u2", "s3", "oc",
)


def dot(a, b, contract, precision=None):
    return lax.dot_general(
        a, b, (contract, ((), ())), precision=precision, preferred_element_type=F32
    )


def split(value):
    high = value.astype(BF16)
    return high, (value - high.astype(F32)).astype(BF16)


def aligned(start, size, unit=8):
    return pl.ds(pl.multiple_of(start, unit), size)


def snp_tables(counts):
    frequency = counts.astype(F32) / (2.0 * COHORT)
    spread = lax.rsqrt(2.0 * frequency * (1.0 - frequency))
    return frequency, spread


def exchange_kernel(
    counts_ref,
    geno_ref,
    traits_ref,
    rel_ref,
    rel,
    projected_ref,
    cross_ref,
    counts,
    traits,
    rowp,
    colp,
    tp,
    tr,
    turned,
    tb,
    rh,
    rl,
    zbuf,
    zsum,
    rsx,
    rsz,
    gsrc,
    gk,
    ga,
    g7,
    gz,
    gx,
    gres,
    csrc,
    c16,
    cc,
    cres,
    ssem,
    rsem,
    lsem,
):
    r = lax.axis_index("row")
    c = lax.axis_index("col")
    y, zl, core = r // 4, (r // 2) % 2, r % 2
    x, zh = c // 4, c % 4

    def row_of(y_, zl_, core_):
        return y_ * 4 + zl_ * 2 + core_

    def at_x(step):
        return (r, ((x + step) % 4) * 4 + zh)

    def at_z(step):
        return (r, x * 4 + (zh + step) % 4)

    def at_y(dy, dl):
        return (row_of((y + dy) % 4, (zl + dl) % 2, core), c)

    sibling = (row_of(y, zl, 1 - core), c)
    mirror = (c, r)
    others = [(dy, dl) for dl in range(2) for dy in range(4) if (dy, dl) != (0, 0)]

    def at_row(dy, dl, dk):
        return (row_of((y + dy) % 4, (zl + dl) % 2, (core + dk) % 2), c)

    def at_col(dx, dz):
        return (r, ((x + dx) % 4) * 4 + (zh + dz) % 4)

    row_others = [
        (dy, dl, dk) for dk in range(2) for dl in range(2) for dy in range(4)
    ][1:]
    col_others = [(dx, dz) for dz in range(4) for dx in range(4)][1:]
    partners = (
        [at_row(*d) for d in row_others]
        + [at_x(i) for i in (1, 2, 3)]
        + [at_z(i) for i in (1, 2, 3)]
    )
    far = r != c

    names = itertools.count()
    started = []

    def copy(number, src, dst, to):
        return pltpu.make_async_remote_copy(
            src_ref=src,
            dst_ref=dst,
            send_sem=ssem.at[number],
            recv_sem=rsem.at[number],
            device_id=to,
            device_id_type=MESH,
        )

    def send(src, dst, to):
        number = next(names)
        moved = copy(number, src, dst, to)
        moved.start()
        started.append(moved)
        return number

    def arrived(number, landing):
        copy(number, landing, landing, sibling).wait_recv()

    load_counts = pltpu.make_async_copy(counts_ref, counts, lsem.at[4])
    load_counts.start()
    load_traits = pltpu.make_async_copy(traits_ref, traits, lsem.at[5])
    load_traits.start()
    keep_own = pltpu.make_async_copy(geno_ref, rowp.at[c], lsem.at[1])
    keep_own.start()
    load_rel = pltpu.make_async_copy(rel_ref, rel, lsem.at[0])
    load_rel.start()

    barrier = pltpu.get_barrier_semaphore()
    for to in partners:
        pl.semaphore_signal(barrier, inc=1, device_id=to, device_id_type=MESH)

    @pl.when(far)
    def _():
        pl.semaphore_signal(barrier, inc=1, device_id=mirror, device_id_type=MESH)

    load_counts.wait()
    frequency, spread = snp_tables(counts[...])
    nearest = jnp.round(2.0 * frequency)
    offset = 2.0 * frequency - nearest
    weight = spread * spread * (1.0 / SNPS)
    keep_own.wait()
    load_traits.wait()
    scores = (rowp[c].astype(F32) - 2.0 * frequency) * spread
    gsrc[...] = dot(traits[...], scores, ((0,), (0,)), HIGHEST)

    pl.semaphore_wait(barrier, len(partners) + far.astype(jnp.int32))

    steps = {}

    def step(function):
        steps[function.__name__] = function

    m_traits, m_geno = next(names), next(names)
    mirrors = {
        "t": (m_traits, traits_ref, lambda i: tp.at[i], 2),
        "c": (m_geno, geno_ref, lambda i: cblock(i), 3),
    }

    def cblock(index):
        return colp.at[aligned(index * ROWS, ROWS)]

    def mirror_start(which):
        number, src, panel, sem = mirrors[which]

        @pl.when(far)
        def _():
            copy(number, src, panel(c), mirror).start()

        @pl.when(jnp.logical_not(far))
        def _():
            pltpu.make_async_copy(src, panel(c), lsem.at[sem]).start()

    def mirrored(which):
        number, src, panel, sem = mirrors[which]

        @pl.when(far)
        def _():
            copy(number, src, panel(r), mirror).wait_recv()

        @pl.when(jnp.logical_not(far))
        def _():
            pltpu.make_async_copy(src, panel(r), lsem.at[sem]).wait()

    def mirror_sent(which):
        number, src, panel, sem = mirrors[which]

        @pl.when(far)
        def _():
            copy(number, src, panel(c), mirror).wait_send()

    class Total:
        def __init__(self, src, bk, acc, b7, bz, bx, res, halves):
            self.src, self.bk, self.acc, self.b7 = src, bk, acc, b7
            self.bz, self.bx, self.res = bz, bx, res
            self.halves = halves
            self.rows = 64 if halves else 128
            self.chunk = self.rows // 8
            self.base = core * 64 if halves else 0

        def part(self, index):
            return aligned(index * self.chunk, self.chunk)

        def to_core(self):
            first = (1 - core) * 64 if self.halves else 0
            self.n_core = send(self.src.at[aligned(first, self.rows)], self.bk, sibling)

        def to_row(self):
            arrived(self.n_core, self.bk)
            mine = self.src[aligned(self.base, self.rows), :]
            self.acc[...] = mine + self.bk[...]
            me = y * 2 + zl
            self.n_row = []
            for dy, dl in others:
                q = ((y + dy) % 4) * 2 + (zl + dl) % 2
                self.n_row.append(
                    send(self.acc.at[self.part(q)], self.b7.at[me], at_y(dy, dl))
                )

        def to_z(self):
            me = y * 2 + zl
            for number in self.n_row:
                arrived(number, self.b7.at[me])
            self.b7[me] = self.acc[self.part(me), :]
            total = self.b7[0]
            for i in range(1, 8):
                total = total + self.b7[i]
            self.bz[zh] = total
            self.n_z = [send(self.bz.at[zh], self.bz.at[zh], at_z(i)) for i in (1, 2, 3)]

        def to_x(self):
            for number in self.n_z:
                arrived(number, self.bz.at[zh])
            total = (self.bz[0] + self.bz[1]) + (self.bz[2] + self.bz[3])
            self.bx[x] = total
            self.n_x = [send(self.bx.at[x], self.bx.at[x], at_x(i)) for i in (1, 2, 3)]

        def back_row(self):
            for number in self.n_x:
                arrived(number, self.bx.at[x])
            total = (self.bx[0] + self.bx[1]) + (self.bx[2] + self.bx[3])
            me = y * 2 + zl
            mine = aligned(self.base + me * self.chunk, self.chunk)
            self.res[mine, :] = total
            self.n_back = [
                send(self.res.at[mine], self.res.at[mine], at_y(dy, dl)) for dy, dl in others
            ]

        def back_core(self):
            me = y * 2 + zl
            mine = aligned(self.base + me * self.chunk, self.chunk)
            for number in self.n_back:
                arrived(number, self.res.at[mine])
            if self.halves:
                half = aligned(self.base, 64)
                self.n_half = send(self.res.at[half], self.res.at[half], sibling)

        def done(self):
            if self.halves:
                arrived(self.n_half, self.res.at[aligned(self.base, 64)])

    gram = Total(gsrc, gk, ga, g7, gz, gx, gres, True)

    class Quick:
        def __init__(self, src, by_row, by_col, res):
            self.src, self.by_row, self.by_col, self.res = src, by_row, by_col, res

        def part(self, index):
            return aligned(index * 8, 8)

        def to_row(self):
            self.n = []
            for d in row_others:
                there = at_row(*d)
                self.n.append(
                    send(self.src.at[self.part(there[0])], self.by_row.at[r], there)
                )
            self.by_row[r] = self.src[self.part(r), :]

        def to_col(self):
            for number in self.n:
                arrived(number, self.by_row.at[r])
            total = self.by_row[0]
            for i in range(1, 16):
                total = total + self.by_row[i]
            self.by_col[c] = total
            mine = self.by_col.at[c]
            self.n = [send(mine, mine, at_col(*d)) for d in col_others]

        def back(self):
            for number in self.n:
                arrived(number, self.by_col.at[c])
            total = self.by_col[0]
            for i in range(1, 16):
                total = total + self.by_col[i]
            self.res[self.part(r), :] = total
            mine = self.res.at[self.part(r)]
            self.n = [send(mine, mine, at_row(*d)) for d in row_others]

        def done(self):
            for number in self.n:
                arrived(number, self.res.at[self.part(r)])

    quick = Quick(csrc, c16, cc, cres)
    steps["s0"], steps["s1"], steps["s2"], steps["s3"] = (
        quick.to_row,
        quick.to_col,
        quick.back,
        quick.done,
    )
    for index, name in enumerate(
        ("to_core", "to_row", "to_z", "to_x", "back_row", "back_core", "done")
    ):
        steps[f"g{index}"] = getattr(gram, name)

    def slot(x_step, z_step):
        return ((x + x_step) % 4) * 4 + (zh + z_step) % 4

    n_z = {}
    n_xup, n_xdown, n_xfup, n_xfdown = {}, {}, {}, {}

    def x_send(k, src):
        there = rowp.at[slot(0, k)]
        n_xup[k] = send(src, there, at_x(1))
        n_xdown[k] = send(src, there, at_x(3))

    def x_up(k):
        low = rowp.at[slot(3, k)]
        arrived(n_xup[k], low)
        n_xfup[k] = send(low.at[0:TOP], low.at[0:TOP], at_x(1))

    def x_down(k):
        high = rowp.at[slot(1, k)]
        arrived(n_xdown[k], high)
        n_xfdown[k] = send(high.at[TOP:ROWS], high.at[TOP:ROWS], at_x(3))

    def x_last(k):
        opposite = rowp.at[slot(2, k)]
        arrived(n_xfup[k], opposite.at[0:TOP])
        arrived(n_xfdown[k], opposite.at[TOP:ROWS])

    for k in range(4):
        steps[f"xf{k}u"] = lambda k=k: x_up(k)
        steps[f"xf{k}d"] = lambda k=k: x_down(k)
        steps[f"xl{k}"] = lambda k=k: x_last(k)

    @step
    def z0():
        n_z["up"] = send(geno_ref, rowp.at[c], at_z(1))
        n_z["down"] = send(geno_ref, rowp.at[c], at_z(3))

    @step
    def x0():
        x_send(0, geno_ref)

    @step
    def z1u():
        low = rowp.at[slot(0, 3)]
        arrived(n_z["up"], low)
        n_z["fup"] = send(low.at[0:TOP], low.at[0:TOP], at_z(1))

    @step
    def z1d():
        high = rowp.at[slot(0, 1)]
        arrived(n_z["down"], high)
        n_z["fdown"] = send(high.at[TOP:ROWS], high.at[TOP:ROWS], at_z(3))

    @step
    def z2():
        opposite = rowp.at[slot(0, 2)]
        arrived(n_z["fup"], opposite.at[0:TOP])
        arrived(n_z["fdown"], opposite.at[TOP:ROWS])

    for k in (1, 2, 3):
        steps[f"x{k}s"] = lambda k=k: x_send(k, rowp.at[slot(0, k)])

    def cslot(dy, dl, other=0):
        return row_of((y + dy) % 4, (zl + dl) % 2, (core + other) % 2)

    n_yup, n_ydown, n_yfup, n_yfdown, n_pair = {}, {}, {}, {}, {}
    n_zl = []

    def pair_send(dy, dl):
        block = cblock(cslot(dy, dl))
        n_pair[dy, dl] = send(block, block, sibling)

    def y_send(dl):
        block = cblock(cslot(0, dl))
        n_yup[dl] = send(block, block, at_y(1, 0))
        n_ydown[dl] = send(block, block, at_y(3, 0))

    def y_up(dl):
        low = cblock(cslot(3, dl))
        arrived(n_yup[dl], low)
        n_yfup[dl] = send(low.at[0:TOP], low.at[0:TOP], at_y(1, 0))

    def y_down(dl):
        high = cblock(cslot(1, dl))
        arrived(n_ydown[dl], high)
        n_yfdown[dl] = send(high.at[TOP:ROWS], high.at[TOP:ROWS], at_y(3, 0))

    def y_last(dl):
        opposite = cblock(cslot(2, dl))
        arrived(n_yfup[dl], opposite.at[0:TOP])
        arrived(n_yfdown[dl], opposite.at[TOP:ROWS])

    for dl in range(2):
        steps[f"ys{dl}"] = lambda dl=dl: y_send(dl)
        for dy in range(4):
            steps[f"pp{dy}{dl}"] = lambda dy=dy, dl=dl: pair_send(dy, dl)
        steps[f"yf{dl}u"] = lambda dl=dl: y_up(dl)
        steps[f"yf{dl}d"] = lambda dl=dl: y_down(dl)
        steps[f"yl{dl}"] = lambda dl=dl: y_last(dl)

    @step
    def m0():
        mirror_start("c")

    @step
    def m1():
        mirrored("c")
        n_zl.append(send(cblock(r), cblock(r), at_y(0, 1)))

    @step
    def m2():
        arrived(n_zl[0], cblock(cslot(0, 1)))

    @step
    def p():
        for dl in range(2):
            for dy in range(4):
                arrived(n_pair[dy, dl], cblock(cslot(dy, dl, 1)))

    n_t, n_tp, n_tz = [], {}, []

    @step
    def t0():
        mirror_start("t")

    @step
    def tz0():
        for i in (1, 2, 3):
            n_tz.append(send(traits_ref, tr.at[zh], at_z(i)))
        tr[zh] = traits[...]

    @step
    def tz1():
        for number in n_tz:
            arrived(number, tr.at[zh])

    @step
    def t1():
        mirrored("t")
        for dy, dl in others:
            n_t.append(send(tp.at[r], tp.at[r], at_y(dy, dl)))
        n_tp[0, 0] = send(tp.at[r], tp.at[r], sibling)

    def t_pair(begin, end):
        for number, (dy, dl) in list(zip(n_t, others, strict=True))[begin:end]:
            block = tp.at[cslot(-dy, -dl)]
            arrived(number, block)
            n_tp[-dy % 4, dl] = send(block, block, sibling)

    steps["t2a"] = lambda: t_pair(0, 3)
    steps["t2"] = lambda: t_pair(3, 7)

    n_rsx, n_rsz = [], []

    @step
    def t3():
        for (dy, dl), number in n_tp.items():
            arrived(number, tp.at[cslot(dy, dl, 1)])
        t_high, t_low = split(tp[...].reshape(PANEL, PROT))
        tb[:, :PROT] = t_high
        tb[:, PROT:] = t_low

    @step
    def rs():
        load_rel.wait()

        def halve(i, _):
            rows = aligned(i * 144, 144, 16)
            rh[rows, :], rl[rows, :] = split(rel[rows, :])
            return 0

        lax.fori_loop(0, 8, halve, 0)

    def times_traits(i):
        rows = aligned(((x + i) % 4) * GROUP, GROUP, 16)
        both = dot(rh[rows, :], tb[...], ((1,), (0,)))
        product = both[:, :PROT] + both[:, PROT:] + dot(rl[rows, :], tb[:, :PROT], ((1,), (0,)))
        zbuf[rows, :] = product
        if i:
            n_rsx.append(send(zbuf.at[rows], rsx.at[x], at_x(i)))
        else:
            rsx[x] = product

    for i in range(4):
        steps[f"m{i}t"] = lambda i=i: times_traits(i)

    @step
    def t4():
        for number in n_rsx:
            arrived(number, rsx.at[x])
        zsum[...] = (rsx[0] + rsx[1]) + (rsx[2] + rsx[3])
        for i in (1, 2, 3):
            rows = aligned(((zh + i) % 4) * ROWS, ROWS)
            n_rsz.append(send(zsum.at[rows], rsz.at[zh], at_z(i)))
        rsz[zh] = zsum[aligned(zh * ROWS, ROWS), :]

    @step
    def tc():
        four = tr[...].reshape(GROUP, PROT)
        csrc[...] = dot(four, zsum[...], ((0,), (0,)), HIGHEST)

    @step
    def h():
        def plain(step, _):
            rows = aligned(step * 128, 128)
            block = (colp[rows, :].astype(F32) - nearest).T
            turned[:, rows] = block.astype(BF16)
            return 0

        lax.fori_loop(0, PANEL // 128, plain, 0)

    def update(i):
        which = (x + i) % 4
        rows = aligned(which * GROUP, GROUP)
        block = rowp[pl.ds(4 * which, 4)].reshape(GROUP, SNPS).astype(F32)
        value = ((block - nearest) - offset) * weight
        high, low = split(value)
        shift = jnp.sum(value * offset, axis=1, keepdims=True)
        sums = dot(high, turned[...], ((1,), (0,))) + dot(low, turned[...], ((1,), (0,)))
        rel[rows, :] = rel[rows, :] + (sums - shift)

    for k in range(4):
        steps[f"u{k}"] = lambda k=k: update(k)

    @step
    def op():
        for number in n_rsz:
            arrived(number, rsz.at[zh])
        own = (rsz[0] + rsz[1]) + (rsz[2] + rsz[3])
        product = own + dot(scores, gres[...], ((1,), (1,)), HIGHEST) * (1.0 / SNPS)
        projected_ref[...] = product * math.sqrt(SNPS / SAMPLES)

    @step
    def og():
        whole = gres[...]
        cross_ref[...] = dot(whole, whole, ((1,), (1,)), HIGHEST) * (1.0 / SNPS)

    @step
    def oc():
        cross_ref[...] = (cres[...] + cross_ref[...]) * (1.0 / SAMPLES)

    order = ORDER
    for name in order:
        steps[name]()

    for moved in started:
        moved.wait_send()
    mirror_sent("t")
    mirror_sent("c")


def store_kernel(updated_ref, projected_ref, cross_ref, out_ref, proj_ref, cp_ref, sem):
    tile = PANEL // STORES
    moves = [
        pltpu.make_async_copy(projected_ref, proj_ref, sem.at[STORES]),
        pltpu.make_async_copy(cross_ref, cp_ref, sem.at[STORES + 1]),
    ]
    for i in range(STORES):
        rows = pl.ds(i * tile, tile)
        moves.append(pltpu.make_async_copy(updated_ref.at[rows], out_ref.at[rows], sem.at[i]))
    for move in moves:
        move.start()
    for move in moves:
        move.wait()


def on_device(genotypes, allele_counts, relatedness, protein_traits):
    vmem = pl.BlockSpec(memory_space=pltpu.VMEM)
    anywhere = pl.BlockSpec(memory_space=pl.ANY)
    like = jax.ShapeDtypeStruct
    f32 = lambda *shape: pltpu.VMEM(shape, F32)
    updated, projected, cross = pl.pallas_call(
        exchange_kernel,
        out_shape=(f32(PANEL, PANEL), f32(ROWS, PROT), f32(PROT, PROT)),
        in_specs=[anywhere] * 4,
        out_specs=(vmem,) * 3,
        scratch_shapes=[
            pltpu.VMEM((1, SNPS), jnp.int32),
            f32(ROWS, PROT),
            pltpu.VMEM((16, ROWS, SNPS), jnp.int32),
            pltpu.VMEM((PANEL, SNPS), jnp.int32),
            f32(16, ROWS, PROT),
            f32(4, ROWS, PROT),
            pltpu.VMEM((SNPS, PANEL), BF16),
            pltpu.VMEM((PANEL, 2 * PROT), BF16),
            pltpu.VMEM((PANEL, PANEL), BF16),
            pltpu.VMEM((PANEL, PANEL), BF16),
            f32(PANEL, PROT),
            f32(GROUP, PROT),
            f32(4, GROUP, PROT),
            f32(4, ROWS, PROT),
            f32(128, SNPS),
            f32(64, SNPS),
            f32(64, SNPS),
            f32(8, 8, SNPS),
            f32(4, 8, SNPS),
            f32(4, 8, SNPS),
            f32(128, SNPS),
            f32(PROT, PROT),
            f32(16, 8, PROT),
            f32(16, 8, PROT),
            f32(PROT, PROT),
            pltpu.SemaphoreType.DMA((NSEM,)),
            pltpu.SemaphoreType.DMA((NSEM,)),
            pltpu.SemaphoreType.DMA((6,)),
        ],
        compiler_params=pltpu.CompilerParams(
            collective_id=1, has_side_effects=True, vmem_limit_bytes=VMEM_LIMIT
        ),
        name="exchange",
    )(allele_counts.reshape(1, SNPS), genotypes, protein_traits, relatedness)
    return pl.pallas_call(
        store_kernel,
        out_shape=(
            like((PANEL, PANEL), F32),
            like((ROWS, PROT), F32),
            like((PROT, PROT), F32),
        ),
        in_specs=[vmem] * 3,
        out_specs=(anywhere,) * 3,
        scratch_shapes=[pltpu.SemaphoreType.DMA((STORES + 2,))],
        compiler_params=pltpu.CompilerParams(vmem_limit_bytes=16 * 2**20),
        name="store",
    )(updated, projected, cross)


def solution(mesh):
    in_specs = (P(("row", "col"), None), P(), P("row", "col"), P(("row", "col"), None))
    out_specs = (P("row", "col"), P(("row", "col"), None), P())
    return jax.shard_map(
        on_device, mesh=mesh, in_specs=in_specs, out_specs=out_specs, check_vma=False
    )
```

```python
import itertools
import math

import jax
import jax.numpy as jnp
from jax import lax
from jax.experimental import pallas as pl
from jax.experimental.pallas import tpu as pltpu
from jax.sharding import PartitionSpec as P

SNPS = 512
PROT = 128
COHORT = 54208
ROWS = 72
TOP = 40
GROUP = 4 * ROWS
PANEL = 16 * ROWS
SAMPLES = 16 * PANEL
MESH = pl.DeviceIdType.MESH
HIGHEST = lax.Precision.HIGHEST
F32 = jnp.float32
BF16 = jnp.bfloat16
NSEM = 160
STORES = 8
VMEM_LIMIT = 52 * 2**20
ORDER = (
    "t0", "z0", "m0", "g0", "t1", "rs", "x0", "z1u", "g1", "x3s", "m1", "ys0", "t2a", "z1d",
    "x1s", "t2", "yf0d", "g2", "yf0u", "t3", "tz0", "m2t", "m1t", "m3t", "m2", "ys1", "yf1u",
    "xf1u", "yl0", "yf1d", "xf0d", "pp11", "pp20", "m0t", "tz1", "xf3d", "pp31", "pp00", "g3",
    "z2", "pp30", "pp01", "t4", "tc", "s0", "pp10", "yl1", "x2s", "g4", "pp21", "xf1d", "s1",
    "g5", "p", "xf0u", "h", "xl1", "xf3u", "xf2u", "u3", "g6", "op", "xf2d", "u1", "s2", "xl0",
    "u0", "og", "xl3", "xl2", "u2", "s3", "oc",
)


def dot(a, b, contract, precision=None):
    return lax.dot_general(
        a, b, (contract, ((), ())), precision=precision, preferred_element_type=F32
    )


def split(value):
    high = value.astype(BF16)
    return high, (value - high.astype(F32)).astype(BF16)


def aligned(start, size, unit=8):
    return pl.ds(pl.multiple_of(start, unit), size)


def snp_tables(counts):
    frequency = counts.astype(F32) / (2.0 * COHORT)
    spread = lax.rsqrt(2.0 * frequency * (1.0 - frequency))
    return frequency, spread


def exchange_kernel(
    counts_ref,
    geno_ref,
    traits_ref,
    rel_ref,
    rel,
    projected_ref,
    cross_ref,
    counts,
    traits,
    rowp,
    colp,
    tp,
    tr,
    turned,
    tb,
    rh,
    rl,
    zbuf,
    zsum,
    rsx,
    rsz,
    gsrc,
    gk,
    ga,
    g7,
    gz,
    gx,
    gres,
    csrc,
    c16,
    cc,
    cres,
    ssem,
    rsem,
    lsem,
):
    r = lax.axis_index("row")
    c = lax.axis_index("col")
    y, zl, core = r // 4, (r // 2) % 2, r % 2
    x, zh = c // 4, c % 4

    def row_of(y_, zl_, core_):
        return y_ * 4 + zl_ * 2 + core_

    def at_x(step):
        return (r, ((x + step) % 4) * 4 + zh)

    def at_z(step):
        return (r, x * 4 + (zh + step) % 4)

    def at_y(dy, dl):
        return (row_of((y + dy) % 4, (zl + dl) % 2, core), c)

    sibling = (row_of(y, zl, 1 - core), c)
    mirror = (c, r)
    others = [(dy, dl) for dl in range(2) for dy in range(4) if (dy, dl) != (0, 0)]

    def at_row(dy, dl, dk):
        return (row_of((y + dy) % 4, (zl + dl) % 2, (core + dk) % 2), c)

    def at_col(dx, dz):
        return (r, ((x + dx) % 4) * 4 + (zh + dz) % 4)

    far_first = sorted(others, key=lambda d: -min(d[0], 4 - d[0]) - d[1])
    row_others = [
        (dy, dl, dk) for dk in range(2) for dl in range(2) for dy in range(4)
    ][1:]
    col_others = [(dx, dz) for dz in range(4) for dx in range(4)][1:]
    col_others.sort(key=lambda d: -min(d[0], 4 - d[0]) - 2 * min(d[1], 4 - d[1]))
    row_others.sort(key=lambda d: -min(d[0], 4 - d[0]) - d[1])
    partners = (
        [at_row(*d) for d in row_others]
        + [at_x(i) for i in (1, 2, 3)]
        + [at_z(i) for i in (1, 2, 3)]
    )
    far = r != c

    names = itertools.count()
    started = []

    def copy(number, src, dst, to):
        return pltpu.make_async_remote_copy(
            src_ref=src,
            dst_ref=dst,
            send_sem=ssem.at[number],
            recv_sem=rsem.at[number],
            device_id=to,
            device_id_type=MESH,
        )

    def send(src, dst, to):
        number = next(names)
        moved = copy(number, src, dst, to)
        moved.start()
        started.append(moved)
        return number

    def arrived(number, landing):
        copy(number, landing, landing, sibling).wait_recv()

    load_counts = pltpu.make_async_copy(counts_ref, counts, lsem.at[4])
    load_counts.start()
    load_traits = pltpu.make_async_copy(traits_ref, traits, lsem.at[5])
    load_traits.start()
    keep_own = pltpu.make_async_copy(geno_ref, rowp.at[c], lsem.at[1])
    keep_own.start()
    load_rel = pltpu.make_async_copy(rel_ref, rel, lsem.at[0])
    load_rel.start()

    barrier = pltpu.get_barrier_semaphore()
    for to in partners:
        pl.semaphore_signal(barrier, inc=1, device_id=to, device_id_type=MESH)

    @pl.when(far)
    def _():
        pl.semaphore_signal(barrier, inc=1, device_id=mirror, device_id_type=MESH)

    load_counts.wait()
    frequency, spread = snp_tables(counts[...])
    nearest = jnp.round(2.0 * frequency)
    offset = 2.0 * frequency - nearest
    weight = spread * spread * (1.0 / SNPS)
    keep_own.wait()
    load_traits.wait()
    scores = (rowp[c].astype(F32) - 2.0 * frequency) * spread
    gsrc[...] = dot(traits[...], scores, ((0,), (0,)), HIGHEST)

    pl.semaphore_wait(barrier, len(partners) + far.astype(jnp.int32))

    steps = {}

    def step(function):
        steps[function.__name__] = function

    m_traits, m_geno = next(names), next(names)
    mirrors = {
        "t": (m_traits, traits_ref, lambda i: tp.at[i], 2),
        "c": (m_geno, geno_ref, lambda i: cblock(i), 3),
    }

    def cblock(index):
        return colp.at[aligned(index * ROWS, ROWS)]

    def mirror_start(which):
        number, src, panel, sem = mirrors[which]

        @pl.when(far)
        def _():
            copy(number, src, panel(c), mirror).start()

        @pl.when(jnp.logical_not(far))
        def _():
            pltpu.make_async_copy(src, panel(c), lsem.at[sem]).start()

    def mirrored(which):
        number, src, panel, sem = mirrors[which]

        @pl.when(far)
        def _():
            copy(number, src, panel(r), mirror).wait_recv()

        @pl.when(jnp.logical_not(far))
        def _():
            pltpu.make_async_copy(src, panel(r), lsem.at[sem]).wait()

    def mirror_sent(which):
        number, src, panel, sem = mirrors[which]

        @pl.when(far)
        def _():
            copy(number, src, panel(c), mirror).wait_send()

    class Total:
        def __init__(self, src, bk, acc, b7, bz, bx, res, halves):
            self.src, self.bk, self.acc, self.b7 = src, bk, acc, b7
            self.bz, self.bx, self.res = bz, bx, res
            self.halves = halves
            self.rows = 64 if halves else 128
            self.chunk = self.rows // 8
            self.base = core * 64 if halves else 0

        def part(self, index):
            return aligned(index * self.chunk, self.chunk)

        def to_core(self):
            first = (1 - core) * 64 if self.halves else 0
            self.n_core = send(self.src.at[aligned(first, self.rows)], self.bk, sibling)

        def to_row(self):
            arrived(self.n_core, self.bk)
            mine = self.src[aligned(self.base, self.rows), :]
            self.acc[...] = mine + self.bk[...]
            me = y * 2 + zl
            self.n_row = []
            for dy, dl in far_first:
                q = ((y + dy) % 4) * 2 + (zl + dl) % 2
                self.n_row.append(
                    send(self.acc.at[self.part(q)], self.b7.at[me], at_y(dy, dl))
                )

        def to_z(self):
            me = y * 2 + zl
            for number in self.n_row:
                arrived(number, self.b7.at[me])
            self.b7[me] = self.acc[self.part(me), :]
            total = self.b7[0]
            for i in range(1, 8):
                total = total + self.b7[i]
            self.bz[zh] = total
            self.n_z = [send(self.bz.at[zh], self.bz.at[zh], at_z(i)) for i in (2, 1, 3)]

        def to_x(self):
            for number in self.n_z:
                arrived(number, self.bz.at[zh])
            total = (self.bz[0] + self.bz[1]) + (self.bz[2] + self.bz[3])
            self.bx[x] = total
            self.n_x = [send(self.bx.at[x], self.bx.at[x], at_x(i)) for i in (2, 1, 3)]

        def back_row(self):
            for number in self.n_x:
                arrived(number, self.bx.at[x])
            total = (self.bx[0] + self.bx[1]) + (self.bx[2] + self.bx[3])
            me = y * 2 + zl
            mine = aligned(self.base + me * self.chunk, self.chunk)
            self.res[mine, :] = total
            self.n_back = [
                send(self.res.at[mine], self.res.at[mine], at_y(dy, dl)) for dy, dl in far_first
            ]

        def back_core(self):
            me = y * 2 + zl
            mine = aligned(self.base + me * self.chunk, self.chunk)
            for number in self.n_back:
                arrived(number, self.res.at[mine])
            if self.halves:
                half = aligned(self.base, 64)
                self.n_half = send(self.res.at[half], self.res.at[half], sibling)

        def done(self):
            if self.halves:
                arrived(self.n_half, self.res.at[aligned(self.base, 64)])

    gram = Total(gsrc, gk, ga, g7, gz, gx, gres, True)

    class Quick:
        def __init__(self, src, by_row, by_col, res):
            self.src, self.by_row, self.by_col, self.res = src, by_row, by_col, res

        def part(self, index):
            return aligned(index * 8, 8)

        def to_row(self):
            self.n = []
            for d in row_others:
                there = at_row(*d)
                self.n.append(
                    send(self.src.at[self.part(there[0])], self.by_row.at[r], there)
                )
            self.by_row[r] = self.src[self.part(r), :]

        def to_col(self):
            for number in self.n:
                arrived(number, self.by_row.at[r])
            total = self.by_row[0]
            for i in range(1, 16):
                total = total + self.by_row[i]
            self.by_col[c] = total
            mine = self.by_col.at[c]
            self.n = [send(mine, mine, at_col(*d)) for d in col_others]

        def back(self):
            for number in self.n:
                arrived(number, self.by_col.at[c])
            total = self.by_col[0]
            for i in range(1, 16):
                total = total + self.by_col[i]
            self.res[self.part(r), :] = total
            mine = self.res.at[self.part(r)]
            self.n = [send(mine, mine, at_row(*d)) for d in row_others]

        def done(self):
            for number in self.n:
                arrived(number, self.res.at[self.part(r)])

    quick = Quick(csrc, c16, cc, cres)
    steps["s0"], steps["s1"], steps["s2"], steps["s3"] = (
        quick.to_row,
        quick.to_col,
        quick.back,
        quick.done,
    )
    for index, name in enumerate(
        ("to_core", "to_row", "to_z", "to_x", "back_row", "back_core", "done")
    ):
        steps[f"g{index}"] = getattr(gram, name)

    def slot(x_step, z_step):
        return ((x + x_step) % 4) * 4 + (zh + z_step) % 4

    n_z = {}
    n_xup, n_xdown, n_xfup, n_xfdown = {}, {}, {}, {}

    def x_send(k, src):
        there = rowp.at[slot(0, k)]
        n_xup[k] = send(src, there, at_x(1))
        n_xdown[k] = send(src, there, at_x(3))

    def x_up(k):
        low = rowp.at[slot(3, k)]
        arrived(n_xup[k], low)
        n_xfup[k] = send(low.at[0:TOP], low.at[0:TOP], at_x(1))

    def x_down(k):
        high = rowp.at[slot(1, k)]
        arrived(n_xdown[k], high)
        n_xfdown[k] = send(high.at[TOP:ROWS], high.at[TOP:ROWS], at_x(3))

    def x_last(k):
        opposite = rowp.at[slot(2, k)]
        arrived(n_xfup[k], opposite.at[0:TOP])
        arrived(n_xfdown[k], opposite.at[TOP:ROWS])

    for k in range(4):
        steps[f"xf{k}u"] = lambda k=k: x_up(k)
        steps[f"xf{k}d"] = lambda k=k: x_down(k)
        steps[f"xl{k}"] = lambda k=k: x_last(k)

    @step
    def z0():
        n_z["up"] = send(geno_ref, rowp.at[c], at_z(1))
        n_z["down"] = send(geno_ref, rowp.at[c], at_z(3))

    @step
    def x0():
        x_send(0, geno_ref)

    @step
    def z1u():
        low = rowp.at[slot(0, 3)]
        arrived(n_z["up"], low)
        n_z["fup"] = send(low.at[0:TOP], low.at[0:TOP], at_z(1))

    @step
    def z1d():
        high = rowp.at[slot(0, 1)]
        arrived(n_z["down"], high)
        n_z["fdown"] = send(high.at[TOP:ROWS], high.at[TOP:ROWS], at_z(3))

    @step
    def z2():
        opposite = rowp.at[slot(0, 2)]
        arrived(n_z["fup"], opposite.at[0:TOP])
        arrived(n_z["fdown"], opposite.at[TOP:ROWS])

    for k in (1, 2, 3):
        steps[f"x{k}s"] = lambda k=k: x_send(k, rowp.at[slot(0, k)])

    def cslot(dy, dl, other=0):
        return row_of((y + dy) % 4, (zl + dl) % 2, (core + other) % 2)

    n_yup, n_ydown, n_yfup, n_yfdown, n_pair = {}, {}, {}, {}, {}
    n_zl = []

    def pair_send(dy, dl):
        block = cblock(cslot(dy, dl))
        n_pair[dy, dl] = send(block, block, sibling)

    def y_send(dl):
        block = cblock(cslot(0, dl))
        n_yup[dl] = send(block, block, at_y(1, 0))
        n_ydown[dl] = send(block, block, at_y(3, 0))

    def y_up(dl):
        low = cblock(cslot(3, dl))
        arrived(n_yup[dl], low)
        n_yfup[dl] = send(low.at[0:TOP], low.at[0:TOP], at_y(1, 0))

    def y_down(dl):
        high = cblock(cslot(1, dl))
        arrived(n_ydown[dl], high)
        n_yfdown[dl] = send(high.at[TOP:ROWS], high.at[TOP:ROWS], at_y(3, 0))

    def y_last(dl):
        opposite = cblock(cslot(2, dl))
        arrived(n_yfup[dl], opposite.at[0:TOP])
        arrived(n_yfdown[dl], opposite.at[TOP:ROWS])

    for dl in range(2):
        steps[f"ys{dl}"] = lambda dl=dl: y_send(dl)
        for dy in range(4):
            steps[f"pp{dy}{dl}"] = lambda dy=dy, dl=dl: pair_send(dy, dl)
        steps[f"yf{dl}u"] = lambda dl=dl: y_up(dl)
        steps[f"yf{dl}d"] = lambda dl=dl: y_down(dl)
        steps[f"yl{dl}"] = lambda dl=dl: y_last(dl)

    @step
    def m0():
        mirror_start("c")

    @step
    def m1():
        mirrored("c")
        n_zl.append(send(cblock(r), cblock(r), at_y(0, 1)))

    @step
    def m2():
        arrived(n_zl[0], cblock(cslot(0, 1)))

    @step
    def p():
        for dl in range(2):
            for dy in range(4):
                arrived(n_pair[dy, dl], cblock(cslot(dy, dl, 1)))

    n_t, n_tp, n_tz = [], {}, []

    @step
    def t0():
        mirror_start("t")

    @step
    def tz0():
        for i in (2, 1, 3):
            n_tz.append(send(traits_ref, tr.at[zh], at_z(i)))
        tr[zh] = traits[...]

    @step
    def tz1():
        for number in n_tz:
            arrived(number, tr.at[zh])

    @step
    def t1():
        mirrored("t")
        sent = {d: send(tp.at[r], tp.at[r], at_y(*d)) for d in far_first}
        n_t.extend(sent[d] for d in others)
        n_tp[0, 0] = send(tp.at[r], tp.at[r], sibling)

    def t_pair(begin, end):
        for number, (dy, dl) in list(zip(n_t, others, strict=True))[begin:end]:
            block = tp.at[cslot(-dy, -dl)]
            arrived(number, block)
            n_tp[-dy % 4, dl] = send(block, block, sibling)

    steps["t2a"] = lambda: t_pair(0, 3)
    steps["t2"] = lambda: t_pair(3, 7)

    n_rsx, n_rsz = [], []

    @step
    def t3():
        for (dy, dl), number in n_tp.items():
            arrived(number, tp.at[cslot(dy, dl, 1)])
        t_high, t_low = split(tp[...].reshape(PANEL, PROT))
        tb[:, :PROT] = t_high
        tb[:, PROT:] = t_low

    @step
    def rs():
        load_rel.wait()

        def halve(i, _):
            rows = aligned(i * 144, 144, 16)
            rh[rows, :], rl[rows, :] = split(rel[rows, :])
            return 0

        lax.fori_loop(0, 8, halve, 0)

    def times_traits(i):
        rows = aligned(((x + i) % 4) * GROUP, GROUP, 16)
        both = dot(rh[rows, :], tb[...], ((1,), (0,)))
        product = both[:, :PROT] + both[:, PROT:] + dot(rl[rows, :], tb[:, :PROT], ((1,), (0,)))
        zbuf[rows, :] = product
        if i:
            n_rsx.append(send(zbuf.at[rows], rsx.at[x], at_x(i)))
        else:
            rsx[x] = product

    for i in range(4):
        steps[f"m{i}t"] = lambda i=i: times_traits(i)

    @step
    def t4():
        for number in n_rsx:
            arrived(number, rsx.at[x])
        zsum[...] = (rsx[0] + rsx[1]) + (rsx[2] + rsx[3])
        for i in (1, 2, 3):
            rows = aligned(((zh + i) % 4) * ROWS, ROWS)
            n_rsz.append(send(zsum.at[rows], rsz.at[zh], at_z(i)))
        rsz[zh] = zsum[aligned(zh * ROWS, ROWS), :]

    @step
    def tc():
        four = tr[...].reshape(GROUP, PROT)
        csrc[...] = dot(four, zsum[...], ((0,), (0,)), HIGHEST)

    @step
    def h():
        def plain(step, _):
            rows = aligned(step * 128, 128)
            block = (colp[rows, :].astype(F32) - nearest).T
            turned[:, rows] = block.astype(BF16)
            return 0

        lax.fori_loop(0, PANEL // 128, plain, 0)

    def update(i):
        which = (x + i) % 4
        rows = aligned(which * GROUP, GROUP)
        block = rowp[pl.ds(4 * which, 4)].reshape(GROUP, SNPS).astype(F32)
        value = ((block - nearest) - offset) * weight
        high, low = split(value)
        shift = jnp.sum(value * offset, axis=1, keepdims=True)
        sums = dot(high, turned[...], ((1,), (0,))) + dot(low, turned[...], ((1,), (0,)))
        rel[rows, :] = rel[rows, :] + (sums - shift)

    for k in range(4):
        steps[f"u{k}"] = lambda k=k: update(k)

    @step
    def op():
        for number in n_rsz:
            arrived(number, rsz.at[zh])
        own = (rsz[0] + rsz[1]) + (rsz[2] + rsz[3])
        product = own + dot(scores, gres[...], ((1,), (1,)), HIGHEST) * (1.0 / SNPS)
        projected_ref[...] = product * math.sqrt(SNPS / SAMPLES)

    @step
    def og():
        whole = gres[...]
        cross_ref[...] = dot(whole, whole, ((1,), (1,)), HIGHEST) * (1.0 / SNPS)

    @step
    def oc():
        cross_ref[...] = (cres[...] + cross_ref[...]) * (1.0 / SAMPLES)

    order = ORDER
    for name in order:
        steps[name]()

    for moved in started:
        moved.wait_send()
    mirror_sent("t")
    mirror_sent("c")


def store_kernel(updated_ref, projected_ref, cross_ref, out_ref, proj_ref, cp_ref, sem):
    tile = PANEL // STORES
    moves = [
        pltpu.make_async_copy(projected_ref, proj_ref, sem.at[STORES]),
        pltpu.make_async_copy(cross_ref, cp_ref, sem.at[STORES + 1]),
    ]
    for i in range(STORES):
        rows = pl.ds(i * tile, tile)
        moves.append(pltpu.make_async_copy(updated_ref.at[rows], out_ref.at[rows], sem.at[i]))
    for move in moves:
        move.start()
    for move in moves:
        move.wait()


def on_device(genotypes, allele_counts, relatedness, protein_traits):
    vmem = pl.BlockSpec(memory_space=pltpu.VMEM)
    anywhere = pl.BlockSpec(memory_space=pl.ANY)
    like = jax.ShapeDtypeStruct
    f32 = lambda *shape: pltpu.VMEM(shape, F32)
    updated, projected, cross = pl.pallas_call(
        exchange_kernel,
        out_shape=(f32(PANEL, PANEL), f32(ROWS, PROT), f32(PROT, PROT)),
        in_specs=[anywhere] * 4,
        out_specs=(vmem,) * 3,
        scratch_shapes=[
            pltpu.VMEM((1, SNPS), jnp.int32),
            f32(ROWS, PROT),
            pltpu.VMEM((16, ROWS, SNPS), jnp.int32),
            pltpu.VMEM((PANEL, SNPS), jnp.int32),
            f32(16, ROWS, PROT),
            f32(4, ROWS, PROT),
            pltpu.VMEM((SNPS, PANEL), BF16),
            pltpu.VMEM((PANEL, 2 * PROT), BF16),
            pltpu.VMEM((PANEL, PANEL), BF16),
            pltpu.VMEM((PANEL, PANEL), BF16),
            f32(PANEL, PROT),
            f32(GROUP, PROT),
            f32(4, GROUP, PROT),
            f32(4, ROWS, PROT),
            f32(128, SNPS),
            f32(64, SNPS),
            f32(64, SNPS),
            f32(8, 8, SNPS),
            f32(4, 8, SNPS),
            f32(4, 8, SNPS),
            f32(128, SNPS),
            f32(PROT, PROT),
            f32(16, 8, PROT),
            f32(16, 8, PROT),
            f32(PROT, PROT),
            pltpu.SemaphoreType.DMA((NSEM,)),
            pltpu.SemaphoreType.DMA((NSEM,)),
            pltpu.SemaphoreType.DMA((6,)),
        ],
        compiler_params=pltpu.CompilerParams(
            collective_id=1, has_side_effects=True, vmem_limit_bytes=VMEM_LIMIT
        ),
        name="exchange",
    )(allele_counts.reshape(1, SNPS), genotypes, protein_traits, relatedness)
    return pl.pallas_call(
        store_kernel,
        out_shape=(
            like((PANEL, PANEL), F32),
            like((ROWS, PROT), F32),
            like((PROT, PROT), F32),
        ),
        in_specs=[vmem] * 3,
        out_specs=(anywhere,) * 3,
        scratch_shapes=[pltpu.SemaphoreType.DMA((STORES + 2,))],
        compiler_params=pltpu.CompilerParams(vmem_limit_bytes=16 * 2**20),
        name="store",
    )(updated, projected, cross)


def solution(mesh):
    in_specs = (P(("row", "col"), None), P(), P("row", "col"), P(("row", "col"), None))
    out_specs = (P("row", "col"), P(("row", "col"), None), P())
    return jax.shard_map(
        on_device, mesh=mesh, in_specs=in_specs, out_specs=out_specs, check_vma=False
    )
```

```python
import itertools
import math

import jax
import jax.numpy as jnp
from jax import lax
from jax.experimental import pallas as pl
from jax.experimental.pallas import tpu as pltpu
from jax.sharding import PartitionSpec as P

SNPS = 512
PROT = 128
COHORT = 54208
ROWS = 72
TOP = 40
GROUP = 4 * ROWS
PANEL = 16 * ROWS
SAMPLES = 16 * PANEL
MESH = pl.DeviceIdType.MESH
HIGHEST = lax.Precision.HIGHEST
F32 = jnp.float32
BF16 = jnp.bfloat16
NSEM = 160
STORES = 8
VMEM_LIMIT = 52 * 2**20
ORDER = (
    "t0", "z0", "m0", "g0", "t1", "rs", "x0", "z1u", "g1", "x3s", "m1", "ys0", "t2a", "z1d",
    "x1s", "t2", "yf0d", "g2", "yf0u", "t3", "tz0", "m2t", "m1t", "m3t", "m2", "ys1", "yf1u",
    "xf1u", "yl0", "yf1d", "xf0d", "pp11", "pp20", "m0t", "tz1", "xf3d", "pp31", "pp00", "g3",
    "z2", "pp30", "pp01", "t4", "tc", "s0", "pp10", "yl1", "x2s", "g4", "pp21", "xf1d", "s1",
    "g5", "p", "xf0u", "h", "xl1", "xf3u", "xf2u", "xf2d", "u3", "g6", "op", "u1", "s2", "xl0",
    "u0", "og", "xl3", "xl2", "u2", "s3", "oc",
)


def dot(a, b, contract, precision=None):
    return lax.dot_general(
        a, b, (contract, ((), ())), precision=precision, preferred_element_type=F32
    )


def split(value):
    high = value.astype(BF16)
    return high, (value - high.astype(F32)).astype(BF16)


def aligned(start, size, unit=8):
    return pl.ds(pl.multiple_of(start, unit), size)


def snp_tables(counts):
    frequency = counts.astype(F32) / (2.0 * COHORT)
    spread = lax.rsqrt(2.0 * frequency * (1.0 - frequency))
    return frequency, spread


def exchange_kernel(
    counts_ref,
    geno_ref,
    traits_ref,
    rel_ref,
    rel,
    projected_ref,
    cross_ref,
    counts,
    traits,
    rowp,
    colp,
    tp,
    tr,
    turned,
    tb,
    rh,
    rl,
    zbuf,
    zsum,
    rsx,
    rsz,
    gsrc,
    gk,
    ga,
    g7,
    gz,
    gx,
    gres,
    csrc,
    c16,
    cc,
    cres,
    ssem,
    rsem,
    lsem,
):
    r = lax.axis_index("row")
    c = lax.axis_index("col")
    y, zl, core = r // 4, (r // 2) % 2, r % 2
    x, zh = c // 4, c % 4

    def row_of(y_, zl_, core_):
        return y_ * 4 + zl_ * 2 + core_

    def at_x(step):
        return (r, ((x + step) % 4) * 4 + zh)

    def at_z(step):
        return (r, x * 4 + (zh + step) % 4)

    def at_y(dy, dl):
        return (row_of((y + dy) % 4, (zl + dl) % 2, core), c)

    sibling = (row_of(y, zl, 1 - core), c)
    mirror = (c, r)
    others = [(dy, dl) for dl in range(2) for dy in range(4) if (dy, dl) != (0, 0)]

    def at_row(dy, dl, dk):
        return (row_of((y + dy) % 4, (zl + dl) % 2, (core + dk) % 2), c)

    def at_col(dx, dz):
        return (r, ((x + dx) % 4) * 4 + (zh + dz) % 4)

    far_first = sorted(others, key=lambda d: -min(d[0], 4 - d[0]) - d[1])
    row_others = [
        (dy, dl, dk) for dk in range(2) for dl in range(2) for dy in range(4)
    ][1:]
    col_others = [(dx, dz) for dz in range(4) for dx in range(4)][1:]
    col_others.sort(key=lambda d: -min(d[0], 4 - d[0]) - 2 * min(d[1], 4 - d[1]))
    row_others.sort(key=lambda d: -min(d[0], 4 - d[0]) - d[1])
    partners = (
        [at_row(*d) for d in row_others]
        + [at_x(i) for i in (1, 2, 3)]
        + [at_z(i) for i in (1, 2, 3)]
    )
    far = r != c

    names = itertools.count()
    started = []

    def copy(number, src, dst, to):
        return pltpu.make_async_remote_copy(
            src_ref=src,
            dst_ref=dst,
            send_sem=ssem.at[number],
            recv_sem=rsem.at[number],
            device_id=to,
            device_id_type=MESH,
        )

    def send(src, dst, to):
        number = next(names)
        moved = copy(number, src, dst, to)
        moved.start()
        started.append(moved)
        return number

    def arrived(number, landing):
        copy(number, landing, landing, sibling).wait_recv()

    load_counts = pltpu.make_async_copy(counts_ref, counts, lsem.at[4])
    load_counts.start()
    load_traits = pltpu.make_async_copy(traits_ref, traits, lsem.at[5])
    load_traits.start()
    keep_own = pltpu.make_async_copy(geno_ref, rowp.at[c], lsem.at[1])
    keep_own.start()
    load_rel = pltpu.make_async_copy(rel_ref, rel, lsem.at[0])
    load_rel.start()

    barrier = pltpu.get_barrier_semaphore()
    for to in partners:
        pl.semaphore_signal(barrier, inc=1, device_id=to, device_id_type=MESH)

    @pl.when(far)
    def _():
        pl.semaphore_signal(barrier, inc=1, device_id=mirror, device_id_type=MESH)

    load_counts.wait()
    frequency, spread = snp_tables(counts[...])
    nearest = jnp.round(2.0 * frequency)
    offset = 2.0 * frequency - nearest
    weight = spread * spread * (1.0 / SNPS)
    keep_own.wait()
    load_traits.wait()
    scores = (rowp[c].astype(F32) - 2.0 * frequency) * spread
    gsrc[...] = dot(traits[...], scores, ((0,), (0,)), HIGHEST)

    pl.semaphore_wait(barrier, len(partners) + far.astype(jnp.int32))

    steps = {}

    def step(function):
        steps[function.__name__] = function

    m_traits, m_geno = next(names), next(names)
    mirrors = {
        "t": (m_traits, traits_ref, lambda i: tp.at[i], 2),
        "c": (m_geno, geno_ref, lambda i: cblock(i), 3),
    }

    def cblock(index):
        return colp.at[aligned(index * ROWS, ROWS)]

    def mirror_start(which):
        number, src, panel, sem = mirrors[which]

        @pl.when(far)
        def _():
            copy(number, src, panel(c), mirror).start()

        @pl.when(jnp.logical_not(far))
        def _():
            pltpu.make_async_copy(src, panel(c), lsem.at[sem]).start()

    def mirrored(which):
        number, src, panel, sem = mirrors[which]

        @pl.when(far)
        def _():
            copy(number, src, panel(r), mirror).wait_recv()

        @pl.when(jnp.logical_not(far))
        def _():
            pltpu.make_async_copy(src, panel(r), lsem.at[sem]).wait()

    def mirror_sent(which):
        number, src, panel, sem = mirrors[which]

        @pl.when(far)
        def _():
            copy(number, src, panel(c), mirror).wait_send()

    class Total:
        def __init__(self, src, bk, acc, b7, bz, bx, res, halves):
            self.src, self.bk, self.acc, self.b7 = src, bk, acc, b7
            self.bz, self.bx, self.res = bz, bx, res
            self.halves = halves
            self.rows = 64 if halves else 128
            self.chunk = self.rows // 8
            self.base = core * 64 if halves else 0

        def part(self, index):
            return aligned(index * self.chunk, self.chunk)

        def to_core(self):
            first = (1 - core) * 64 if self.halves else 0
            self.n_core = send(self.src.at[aligned(first, self.rows)], self.bk, sibling)

        def to_row(self):
            arrived(self.n_core, self.bk)
            mine = self.src[aligned(self.base, self.rows), :]
            self.acc[...] = mine + self.bk[...]
            me = y * 2 + zl
            self.n_row = []
            for dy, dl in far_first:
                q = ((y + dy) % 4) * 2 + (zl + dl) % 2
                self.n_row.append(
                    send(self.acc.at[self.part(q)], self.b7.at[me], at_y(dy, dl))
                )

        def to_z(self):
            me = y * 2 + zl
            for number in self.n_row:
                arrived(number, self.b7.at[me])
            self.b7[me] = self.acc[self.part(me), :]
            total = self.b7[0]
            for i in range(1, 8):
                total = total + self.b7[i]
            self.bz[zh] = total
            self.n_z = [send(self.bz.at[zh], self.bz.at[zh], at_z(i)) for i in (2, 1, 3)]

        def to_x(self):
            for number in self.n_z:
                arrived(number, self.bz.at[zh])
            total = (self.bz[0] + self.bz[1]) + (self.bz[2] + self.bz[3])
            self.bx[x] = total
            self.n_x = [send(self.bx.at[x], self.bx.at[x], at_x(i)) for i in (2, 1, 3)]

        def back_row(self):
            for number in self.n_x:
                arrived(number, self.bx.at[x])
            total = (self.bx[0] + self.bx[1]) + (self.bx[2] + self.bx[3])
            me = y * 2 + zl
            mine = aligned(self.base + me * self.chunk, self.chunk)
            self.res[mine, :] = total
            self.n_back = [
                send(self.res.at[mine], self.res.at[mine], at_y(dy, dl)) for dy, dl in far_first
            ]

        def back_core(self):
            me = y * 2 + zl
            mine = aligned(self.base + me * self.chunk, self.chunk)
            for number in self.n_back:
                arrived(number, self.res.at[mine])
            if self.halves:
                half = aligned(self.base, 64)
                self.n_half = send(self.res.at[half], self.res.at[half], sibling)

        def done(self):
            if self.halves:
                arrived(self.n_half, self.res.at[aligned(self.base, 64)])

    gram = Total(gsrc, gk, ga, g7, gz, gx, gres, True)

    class Quick:
        def __init__(self, src, by_row, by_col, res):
            self.src, self.by_row, self.by_col, self.res = src, by_row, by_col, res

        def part(self, index):
            return aligned(index * 8, 8)

        def to_row(self):
            self.n = []
            for d in row_others:
                there = at_row(*d)
                self.n.append(
                    send(self.src.at[self.part(there[0])], self.by_row.at[r], there)
                )
            self.by_row[r] = self.src[self.part(r), :]

        def to_col(self):
            for number in self.n:
                arrived(number, self.by_row.at[r])
            total = self.by_row[0]
            for i in range(1, 16):
                total = total + self.by_row[i]
            self.by_col[c] = total
            mine = self.by_col.at[c]
            self.n = [send(mine, mine, at_col(*d)) for d in col_others]

        def back(self):
            for number in self.n:
                arrived(number, self.by_col.at[c])
            total = self.by_col[0]
            for i in range(1, 16):
                total = total + self.by_col[i]
            self.res[self.part(r), :] = total
            mine = self.res.at[self.part(r)]
            self.n = [send(mine, mine, at_row(*d)) for d in row_others]

        def done(self):
            for number in self.n:
                arrived(number, self.res.at[self.part(r)])

    quick = Quick(csrc, c16, cc, cres)
    steps["s0"], steps["s1"], steps["s2"], steps["s3"] = (
        quick.to_row,
        quick.to_col,
        quick.back,
        quick.done,
    )
    for index, name in enumerate(
        ("to_core", "to_row", "to_z", "to_x", "back_row", "back_core", "done")
    ):
        steps[f"g{index}"] = getattr(gram, name)

    def slot(x_step, z_step):
        return ((x + x_step) % 4) * 4 + (zh + z_step) % 4

    n_z = {}
    n_xup, n_xdown, n_xfup, n_xfdown = {}, {}, {}, {}

    def x_send(k, src):
        there = rowp.at[slot(0, k)]
        n_xup[k] = send(src, there, at_x(1))
        n_xdown[k] = send(src, there, at_x(3))

    def x_up(k):
        low = rowp.at[slot(3, k)]
        arrived(n_xup[k], low)
        n_xfup[k] = send(low.at[0:TOP], low.at[0:TOP], at_x(1))

    def x_down(k):
        high = rowp.at[slot(1, k)]
        arrived(n_xdown[k], high)
        n_xfdown[k] = send(high.at[TOP:ROWS], high.at[TOP:ROWS], at_x(3))

    def x_last(k):
        opposite = rowp.at[slot(2, k)]
        arrived(n_xfup[k], opposite.at[0:TOP])
        arrived(n_xfdown[k], opposite.at[TOP:ROWS])

    for k in range(4):
        steps[f"xf{k}u"] = lambda k=k: x_up(k)
        steps[f"xf{k}d"] = lambda k=k: x_down(k)
        steps[f"xl{k}"] = lambda k=k: x_last(k)

    @step
    def z0():
        n_z["up"] = send(geno_ref, rowp.at[c], at_z(1))
        n_z["down"] = send(geno_ref, rowp.at[c], at_z(3))

    @step
    def x0():
        x_send(0, geno_ref)

    @step
    def z1u():
        low = rowp.at[slot(0, 3)]
        arrived(n_z["up"], low)
        n_z["fup"] = send(low.at[0:TOP], low.at[0:TOP], at_z(1))

    @step
    def z1d():
        high = rowp.at[slot(0, 1)]
        arrived(n_z["down"], high)
        n_z["fdown"] = send(high.at[TOP:ROWS], high.at[TOP:ROWS], at_z(3))

    @step
    def z2():
        opposite = rowp.at[slot(0, 2)]
        arrived(n_z["fup"], opposite.at[0:TOP])
        arrived(n_z["fdown"], opposite.at[TOP:ROWS])

    for k in (1, 2, 3):
        steps[f"x{k}s"] = lambda k=k: x_send(k, rowp.at[slot(0, k)])

    def cslot(dy, dl, other=0):
        return row_of((y + dy) % 4, (zl + dl) % 2, (core + other) % 2)

    n_yup, n_ydown, n_yfup, n_yfdown, n_pair = {}, {}, {}, {}, {}
    n_zl = []

    def pair_send(dy, dl):
        block = cblock(cslot(dy, dl))
        n_pair[dy, dl] = send(block, block, sibling)

    def y_send(dl):
        block = cblock(cslot(0, dl))
        n_yup[dl] = send(block, block, at_y(1, 0))
        n_ydown[dl] = send(block, block, at_y(3, 0))

    def y_up(dl):
        low = cblock(cslot(3, dl))
        arrived(n_yup[dl], low)
        n_yfup[dl] = send(low.at[0:TOP], low.at[0:TOP], at_y(1, 0))

    def y_down(dl):
        high = cblock(cslot(1, dl))
        arrived(n_ydown[dl], high)
        n_yfdown[dl] = send(high.at[TOP:ROWS], high.at[TOP:ROWS], at_y(3, 0))

    def y_last(dl):
        opposite = cblock(cslot(2, dl))
        arrived(n_yfup[dl], opposite.at[0:TOP])
        arrived(n_yfdown[dl], opposite.at[TOP:ROWS])

    for dl in range(2):
        steps[f"ys{dl}"] = lambda dl=dl: y_send(dl)
        for dy in range(4):
            steps[f"pp{dy}{dl}"] = lambda dy=dy, dl=dl: pair_send(dy, dl)
        steps[f"yf{dl}u"] = lambda dl=dl: y_up(dl)
        steps[f"yf{dl}d"] = lambda dl=dl: y_down(dl)
        steps[f"yl{dl}"] = lambda dl=dl: y_last(dl)

    @step
    def m0():
        mirror_start("c")

    @step
    def m1():
        mirrored("c")
        n_zl.append(send(cblock(r), cblock(r), at_y(0, 1)))

    @step
    def m2():
        arrived(n_zl[0], cblock(cslot(0, 1)))

    @step
    def p():
        for dl in range(2):
            for dy in range(4):
                arrived(n_pair[dy, dl], cblock(cslot(dy, dl, 1)))

    n_t, n_tp, n_tz = [], {}, []

    @step
    def t0():
        mirror_start("t")

    @step
    def tz0():
        for i in (2, 1, 3):
            n_tz.append(send(traits_ref, tr.at[zh], at_z(i)))
        tr[zh] = traits[...]

    @step
    def tz1():
        for number in n_tz:
            arrived(number, tr.at[zh])

    @step
    def t1():
        mirrored("t")
        sent = {d: send(tp.at[r], tp.at[r], at_y(*d)) for d in far_first}
        n_t.extend(sent[d] for d in others)
        n_tp[0, 0] = send(tp.at[r], tp.at[r], sibling)

    def t_pair(begin, end):
        for number, (dy, dl) in list(zip(n_t, others, strict=True))[begin:end]:
            block = tp.at[cslot(-dy, -dl)]
            arrived(number, block)
            n_tp[-dy % 4, dl] = send(block, block, sibling)

    steps["t2a"] = lambda: t_pair(0, 3)
    steps["t2"] = lambda: t_pair(3, 7)

    n_rsx, n_rsz = [], []

    @step
    def t3():
        for (dy, dl), number in n_tp.items():
            arrived(number, tp.at[cslot(dy, dl, 1)])
        t_high, t_low = split(tp[...].reshape(PANEL, PROT))
        tb[:, :PROT] = t_high
        tb[:, PROT:] = t_low

    @step
    def rs():
        load_rel.wait()

        def halve(i, _):
            rows = aligned(i * 144, 144, 16)
            rh[rows, :], rl[rows, :] = split(rel[rows, :])
            return 0

        lax.fori_loop(0, 8, halve, 0)

    def times_traits(i):
        rows = aligned(((x + i) % 4) * GROUP, GROUP, 16)
        both = dot(rh[rows, :], tb[...], ((1,), (0,)))
        product = both[:, :PROT] + both[:, PROT:] + dot(rl[rows, :], tb[:, :PROT], ((1,), (0,)))
        zbuf[rows, :] = product
        if i:
            n_rsx.append(send(zbuf.at[rows], rsx.at[x], at_x(i)))
        else:
            rsx[x] = product

    for i in range(4):
        steps[f"m{i}t"] = lambda i=i: times_traits(i)

    @step
    def t4():
        for number in n_rsx:
            arrived(number, rsx.at[x])
        zsum[...] = (rsx[0] + rsx[1]) + (rsx[2] + rsx[3])
        for i in (1, 2, 3):
            rows = aligned(((zh + i) % 4) * ROWS, ROWS)
            n_rsz.append(send(zsum.at[rows], rsz.at[zh], at_z(i)))
        rsz[zh] = zsum[aligned(zh * ROWS, ROWS), :]

    @step
    def tc():
        four = tr[...].reshape(GROUP, PROT)
        csrc[...] = dot(four, zsum[...], ((0,), (0,)), HIGHEST)

    @step
    def h():
        def plain(step, _):
            rows = aligned(step * 128, 128)
            block = (colp[rows, :].astype(F32) - nearest).T
            turned[:, rows] = block.astype(BF16)
            return 0

        lax.fori_loop(0, PANEL // 128, plain, 0)

    def update(i):
        which = (x + i) % 4
        rows = aligned(which * GROUP, GROUP)
        block = rowp[pl.ds(4 * which, 4)].reshape(GROUP, SNPS).astype(F32)
        value = ((block - nearest) - offset) * weight
        high, low = split(value)
        shift = jnp.sum(value * offset, axis=1, keepdims=True)
        sums = dot(high, turned[...], ((1,), (0,))) + dot(low, turned[...], ((1,), (0,)))
        rel[rows, :] = rel[rows, :] + (sums - shift)

    for k in range(4):
        steps[f"u{k}"] = lambda k=k: update(k)

    @step
    def op():
        for number in n_rsz:
            arrived(number, rsz.at[zh])
        own = (rsz[0] + rsz[1]) + (rsz[2] + rsz[3])
        product = own + dot(scores, gres[...], ((1,), (1,)), HIGHEST) * (1.0 / SNPS)
        projected_ref[...] = product * math.sqrt(SNPS / SAMPLES)

    @step
    def og():
        whole = gres[...]
        cross_ref[...] = dot(whole, whole, ((1,), (1,)), HIGHEST) * (1.0 / SNPS)

    @step
    def oc():
        cross_ref[...] = (cres[...] + cross_ref[...]) * (1.0 / SAMPLES)

    order = ORDER
    for name in order:
        steps[name]()

    for moved in started:
        moved.wait_send()
    mirror_sent("t")
    mirror_sent("c")


def store_kernel(updated_ref, projected_ref, cross_ref, out_ref, proj_ref, cp_ref, sem):
    tile = PANEL // STORES
    moves = [
        pltpu.make_async_copy(projected_ref, proj_ref, sem.at[STORES]),
        pltpu.make_async_copy(cross_ref, cp_ref, sem.at[STORES + 1]),
    ]
    for i in range(STORES):
        rows = pl.ds(i * tile, tile)
        moves.append(pltpu.make_async_copy(updated_ref.at[rows], out_ref.at[rows], sem.at[i]))
    for move in moves:
        move.start()
    for move in moves:
        move.wait()


def on_device(genotypes, allele_counts, relatedness, protein_traits):
    vmem = pl.BlockSpec(memory_space=pltpu.VMEM)
    anywhere = pl.BlockSpec(memory_space=pl.ANY)
    like = jax.ShapeDtypeStruct
    f32 = lambda *shape: pltpu.VMEM(shape, F32)
    updated, projected, cross = pl.pallas_call(
        exchange_kernel,
        out_shape=(f32(PANEL, PANEL), f32(ROWS, PROT), f32(PROT, PROT)),
        in_specs=[anywhere] * 4,
        out_specs=(vmem,) * 3,
        scratch_shapes=[
            pltpu.VMEM((1, SNPS), jnp.int32),
            f32(ROWS, PROT),
            pltpu.VMEM((16, ROWS, SNPS), jnp.int32),
            pltpu.VMEM((PANEL, SNPS), jnp.int32),
            f32(16, ROWS, PROT),
            f32(4, ROWS, PROT),
            pltpu.VMEM((SNPS, PANEL), BF16),
            pltpu.VMEM((PANEL, 2 * PROT), BF16),
            pltpu.VMEM((PANEL, PANEL), BF16),
            pltpu.VMEM((PANEL, PANEL), BF16),
            f32(PANEL, PROT),
            f32(GROUP, PROT),
            f32(4, GROUP, PROT),
            f32(4, ROWS, PROT),
            f32(128, SNPS),
            f32(64, SNPS),
            f32(64, SNPS),
            f32(8, 8, SNPS),
            f32(4, 8, SNPS),
            f32(4, 8, SNPS),
            f32(128, SNPS),
            f32(PROT, PROT),
            f32(16, 8, PROT),
            f32(16, 8, PROT),
            f32(PROT, PROT),
            pltpu.SemaphoreType.DMA((NSEM,)),
            pltpu.SemaphoreType.DMA((NSEM,)),
            pltpu.SemaphoreType.DMA((6,)),
        ],
        compiler_params=pltpu.CompilerParams(
            collective_id=1, has_side_effects=True, vmem_limit_bytes=VMEM_LIMIT
        ),
        name="exchange",
    )(allele_counts.reshape(1, SNPS), genotypes, protein_traits, relatedness)
    return pl.pallas_call(
        store_kernel,
        out_shape=(
            like((PANEL, PANEL), F32),
            like((ROWS, PROT), F32),
            like((PROT, PROT), F32),
        ),
        in_specs=[vmem] * 3,
        out_specs=(anywhere,) * 3,
        scratch_shapes=[pltpu.SemaphoreType.DMA((STORES + 2,))],
        compiler_params=pltpu.CompilerParams(vmem_limit_bytes=16 * 2**20),
        name="store",
    )(updated, projected, cross)


def solution(mesh):
    in_specs = (P(("row", "col"), None), P(), P("row", "col"), P(("row", "col"), None))
    out_specs = (P("row", "col"), P(("row", "col"), None), P())
    return jax.shard_map(
        on_device, mesh=mesh, in_specs=in_specs, out_specs=out_specs, check_vma=False
    )
```
